32 devices in a mesh: queue: 4 (over z), seq: 8 (over y, x, core).
Axes of the slice: x: 2, y: 2, z: 4, core: 2. Of those that a mesh axis runs over, the one named last changes fastest.
Arguments:
- latents: bfloat16 [4, 8, 128, 3072], P('queue', None, 'seq'), may hold values from -6 to 6
- queries: bfloat16 [4, 8, 128, 3072], P('queue', None, 'seq'), may hold values from -5 to 5
- keys: bfloat16 [4, 8, 128, 3072], P('queue', None, 'seq'), may hold values from -5 to 5
- values: bfloat16 [4, 8, 128, 3072], P('queue', None, 'seq'), may hold values from -6 to 6
- fresh_frames: bfloat16 [2, 128, 3072], P(None, 'seq'), may hold values from -6 to 6
- timesteps: int32 [4], replicated, may hold values from 1 to 32, as said below
- offsets: int32 [4], P('queue'), may hold values from 1 to 2
Outputs:
- attended: bfloat16 [4, 8, 128, 3072], P('queue', None, 'seq')
- advanced: bfloat16 [4, 8, 128, 3072], P('queue', None, 'seq')
The draws below stay inside these ranges and needn't reach their ends.
Inputs may be any that keep to these rules, and one draw needn't show every extreme that they name: `timesteps`: block b has an index from 8 b + 1 to 8 b + 8; the last block has 32.
All inputs are finite; a program needn't handle non-finite values.
Results may differ from the reference program's by a relative error of at most 0.0033.
Values may be sent and summed in bfloat16 or wider, within the bound.
No kernel may reach another device: no remote copies, remote signals or barrier semaphores. Data moves between devices by JAX's collectives and lax.ppermute only.
A program may use at most 64 MiB of HBM per device.

```python
import math
import jax
import jax.numpy as jnp
from jax import lax

HEADS = 24
HEAD_SIZE = 128
D = 3072
FRAMES = 8
MAX_SHIFT = 2
BLOCKS = 4
FT = 128
LEVELS = 32


def shared_pair(key):
    length = FRAMES * FT
    shape = (BLOCKS, length, HEADS, HEAD_SIZE)
    key_scale, key_query, key_key = jax.random.split(jax.random.fold_in(key, 101), 3)
    head_scale = jnp.exp(jax.random.uniform(key_scale, (HEADS, 1), jnp.float32, math.log(0.6), math.log(1.8)))
    normal_query = jax.random.normal(key_query, shape, jnp.float32)
    normal_key = jax.random.normal(key_key, shape, jnp.float32)
    query_base = normal_query
    key_base = normal_key
    query_full = query_base * head_scale
    key_full = key_base * head_scale
    count = max(length // 64, 1)
    marks = jnp.arange(count, dtype=jnp.int32)
    query_spots = (marks * 64 + 3) % length
    key_spots = (query_spots * 5 + 17) % length
    second_spots = (key_spots + length // 2 + 1) % length
    key_full = key_full.at[:, key_spots].set(key_full[:, key_spots])
    key_full = key_full.at[:, second_spots].set(key_full[:, second_spots])
    query_full = query_full.at[:, query_spots].set(query_full[:, query_spots])
    query_full = jnp.clip(query_full, -5.0, 5.0).reshape(BLOCKS, FRAMES, FT, D)
    key_full = jnp.clip(key_full, -5.0, 5.0).reshape(BLOCKS, FRAMES, FT, D)
    return (query_full, key_full)


def draw_queries(key, part):
    paired = shared_pair(key)
    return paired[0].astype(jnp.bfloat16)


def draw_keys(key, part):
    paired = shared_pair(key)
    return paired[1].astype(jnp.bfloat16)


def draw_timesteps(key, part):
    key = jax.random.fold_in(key, 13)
    places = jnp.arange(BLOCKS, dtype=jnp.int32)
    extra = jax.random.randint(key, (BLOCKS,), 0, 8, dtype=jnp.int32)
    steps = 8 * places + 1 + extra
    return jnp.where(places == BLOCKS - 1, 8 * BLOCKS, steps).astype(jnp.int32)


def set_ends(values, key, smallest, high):
    longest = values.shape.index(max(values.shape))
    spots = []
    for shift in (0, 1):
        where = [jax.random.randint(jax.random.fold_in(key, axis), (), 0, length) for axis, length in enumerate(values.shape)]
        where[longest] = (where[longest] + shift) % values.shape[longest]
        spots.append(tuple(where))
    return values.at[spots[0]].set(smallest).at[spots[1]].set(high)


def steps_of(rng, dims, cuts, low, high):
    gain, own = 1.0, jax.random.fold_in(rng, 6)
    for dim, parts in cuts:
        steps = jnp.exp(jax.random.uniform(jax.random.fold_in(own, dim), (parts,), jnp.float32, low / len(cuts), high / len(cuts)))
        gain = gain * jnp.repeat(steps, dims[dim] // parts).reshape([-1 if axis == dim else 1 for axis in range(len(dims))])
    return gain


def centred(rng, extent, width, bound, pieces=(), kind=jnp.bfloat16):
    values = jax.random.normal(rng, extent, jnp.float32) * width
    if len(pieces) > 0:
        values = steps_of(rng, extent, pieces, -0.22, 0.18) * values
    return jnp.clip(values, min=-bound, max=bound).astype(kind)


def setup_inputs(seed: int = 0) -> dict:
    streams_of = jax.random.split(jax.random.key(seed), 8)
    return {
        "latents": centred(streams_of[0], (BLOCKS, FRAMES, FT, D), 1.0, 6.0, ((0, 4), (2, 8))),
        "queries": draw_queries(jax.random.fold_in(streams_of[7], 71), 0),
        "keys": draw_keys(jax.random.fold_in(streams_of[7], 71), 0),
        "values": centred(streams_of[3], (BLOCKS, FRAMES, FT, D), 1.0, 6.0, ((0, 4), (2, 8))),
        "fresh_frames": centred(streams_of[4], (MAX_SHIFT, FT, D), 1.0, 6.0, ((1, 8),)),
        "timesteps": draw_timesteps(jax.random.fold_in(streams_of[7], 71), 0),
        "offsets": set_ends(jax.random.randint(streams_of[6], (BLOCKS,), 1, MAX_SHIFT + 1), jax.random.fold_in(streams_of[6], 1), 1, MAX_SHIFT).astype(jnp.int32),
    }


def level(step, count):
    ratio = step.astype(jnp.float32) / count
    return 7.0 * ratio / (1.0 + 6.0 * ratio)


def attend_head(query_head, key_head, value_head):
    length = query_head.shape[0]
    block = min(512, length)
    scale = HEAD_SIZE ** -0.5

    def one_block(query_block):
        scores = jnp.dot(query_block, key_head.T, preferred_element_type=jnp.float32) * scale
        top = jnp.max(scores, axis=-1, keepdims=True)
        weights = jnp.exp(scores - top)
        total = jnp.sum(weights, axis=-1, keepdims=True)
        mixed = jnp.dot(weights.astype(jnp.bfloat16), value_head, preferred_element_type=jnp.float32) / total
        return mixed.astype(jnp.bfloat16)

    blocks = query_head.reshape(length // block, block, HEAD_SIZE)
    return lax.map(one_block, blocks).reshape(length, HEAD_SIZE)


def attend_block(triple):
    query_blk, key_blk, value_blk = triple
    length = FRAMES * FT
    def heads_first(array):
        return array.reshape(length, HEADS, HEAD_SIZE).transpose(1, 0, 2)
    result = lax.map(lambda group: attend_head(group[0], group[1], group[2]),
                     (heads_first(query_blk), heads_first(key_blk), heads_first(value_blk)))
    return result.transpose(1, 0, 2).reshape(FRAMES, FT, D)


def take_frames(joined_row, start):
    return lax.dynamic_slice_in_dim(joined_row, start, FRAMES, 0)


def reference(latents, queries, keys, values, fresh_frames, timesteps, offsets):
    attended = lax.map(attend_block, (queries, keys, values))
    delta = 8.0 * (level(timesteps - 1, LEVELS) - level(timesteps, LEVELS))
    updated = (latents.astype(jnp.float32) + delta[:, None, None, None] * attended.astype(jnp.float32)).astype(jnp.bfloat16)
    incoming = jnp.concatenate([updated[1:, :MAX_SHIFT], fresh_frames[None]], axis=0)
    joined = jnp.concatenate([updated, incoming], axis=1)
    advanced = jax.vmap(take_frames)(joined, offsets.astype(jnp.int32))
    return attended, advanced
```

```python
import functools
import jax
import jax.numpy as jnp
from jax import lax
from jax.experimental import pallas as pl
from jax.experimental.pallas import tpu as pltpu
from jax.sharding import PartitionSpec as P

HEAD_SIZE = 128
GROUPS = 8
HEAD_GRP = 3
MAX_SHIFT = 2
LOG2E = 1.4426950408889634
CORE, ACROSS, DOWN = 1, 2, 4


def shifted(block, axis, distance):
    devices = range(lax.axis_size(axis))
    route = [(i - distance, i) for i in devices if i - distance in devices]
    return lax.ppermute(block, axis, route)


def swapped(block, bit):
    return lax.ppermute(block, "seq", [(i, i ^ bit) for i in range(lax.axis_size("seq"))])


def level(step, count):
    ratio = step.astype(jnp.float32) / count
    return 7.0 * ratio / (1.0 + 6.0 * ratio)


def advance(latents, attended, fresh_frames, timesteps, offsets):
    queue_count = lax.axis_size("queue")
    position = lax.axis_index("queue")
    frame_count = latents.shape[1]
    level_count = 8 * queue_count
    own_step = lax.dynamic_index_in_dim(timesteps, position, 0, keepdims=False)
    delta = 8.0 * (level(own_step - 1, level_count) - level(own_step, level_count))
    updated = (latents.astype(jnp.float32) + delta * attended.astype(jnp.float32)).astype(
        jnp.bfloat16
    )
    incoming = shifted(updated[:, :MAX_SHIFT], "queue", -1)
    incoming = jnp.where(position == queue_count - 1, fresh_frames[None], incoming)
    joined = jnp.concatenate([updated, incoming], axis=1)
    return lax.dynamic_slice_in_dim(joined, offsets[0], frame_count, 1)


def attend_items(query_part, key_part, value_part):
    length = query_part.shape[0]
    block = min(512, length)
    scale = HEAD_SIZE ** (-0.5)
    results = []
    for item in range(query_part.shape[1]):
        key_head = key_part[:, item]
        value_head = value_part[:, item]

        def one_block(query_block):
            scores = (
                jnp.einsum("qd,kd->qk", query_block, key_head, preferred_element_type=jnp.float32)
                * scale
            )
            top = jnp.max(scores, axis=-1, keepdims=True)
            weights = jnp.exp(scores - top)
            total = jnp.sum(weights, axis=-1, keepdims=True)
            mixed = (
                jnp.dot(
                    weights.astype(jnp.bfloat16), value_head, preferred_element_type=jnp.float32
                )
                / total
            )
            return mixed.astype(jnp.bfloat16)

        blocks = query_part[:, item].reshape(length // block, block, HEAD_SIZE)
        results.append(lax.map(one_block, blocks).reshape(length, HEAD_SIZE))
    return jnp.stack(results, axis=1)


def grouped_shards(latents, queries, keys, values, fresh_frames, timesteps, offsets):
    frame_count = latents.shape[1]
    frame_rows = latents.shape[2]
    seq_count = lax.axis_size("seq")
    quarters = seq_count // GROUPS
    row_count = frame_count * frame_rows
    quarter_rows = row_count // quarters
    quarter = lax.axis_index("seq") // GROUPS
    split_keys = keys.reshape(row_count, 1, GROUPS, HEAD_GRP, 1, HEAD_SIZE)
    split_values = values.reshape(row_count, 1, GROUPS, HEAD_GRP, 1, HEAD_SIZE)
    split_queries = queries.reshape(row_count, 1, GROUPS, HEAD_GRP, 1, HEAD_SIZE)
    triple = jnp.concatenate([split_queries, split_keys, split_values], axis=4)
    triple = jnp.broadcast_to(triple, (row_count, quarters, GROUPS, HEAD_GRP, 3, HEAD_SIZE))
    triple = triple.reshape(row_count, seq_count, HEAD_GRP, 3, HEAD_SIZE)
    piece = lax.all_to_all(triple, "seq", split_axis=1, concat_axis=0, tiled=True)
    items = piece.shape[2]
    query_part = piece[:, 0, :, 0].reshape(seq_count, quarter_rows, quarters, items, HEAD_SIZE)
    query_part = lax.dynamic_index_in_dim(query_part, quarter, 2, keepdims=False)
    query_part = query_part.reshape(seq_count * quarter_rows, items, HEAD_SIZE)
    outcome = attend_items(query_part, piece[:, 0, :, 1], piece[:, 0, :, 2])
    outcome = outcome.reshape(seq_count, quarter_rows, HEAD_GRP * HEAD_SIZE)
    gathered = lax.all_to_all(outcome, "seq", split_axis=0, concat_axis=2, tiled=True)
    attended = gathered.reshape(latents.shape)
    return (attended, advance(latents, attended, fresh_frames, timesteps, offsets))


def attend_kernel(query_ref, near_ref, far_ref, core_ref, core_far_ref, own_ref, back_ref):
    parts = (near_ref, far_ref, core_ref, core_far_ref)
    rows = own_ref.shape[0]
    factor = LOG2E * HEAD_SIZE ** (-0.5)
    for head in range(query_ref.shape[1] // HEAD_SIZE):
        cols = slice(head * HEAD_SIZE, (head + 1) * HEAD_SIZE)
        for out_ref, start in ((own_ref, 0), (back_ref, rows)):
            query = query_ref[start : start + rows, cols]
            scores = [
                lax.dot_general(
                    query,
                    part[0, :, cols],
                    (((1,), (1,)), ((), ())),
                    preferred_element_type=jnp.float32,
                )
                for part in parts
            ]
            top = jnp.maximum(
                jnp.maximum(scores[0], scores[1]), jnp.maximum(scores[2], scores[3])
            )
            top = jnp.max(top, axis=-1, keepdims=True)
            weights = [jnp.exp2((score - top) * factor) for score in scores]
            total = (weights[0] + weights[1]) + (weights[2] + weights[3])
            total = jnp.sum(total, axis=-1, keepdims=True)
            mixed = sum(
                jnp.dot(
                    weight.astype(jnp.bfloat16),
                    part[1, :, cols],
                    preferred_element_type=jnp.float32,
                )
                for weight, part in zip(weights, parts)
            )
            out_ref[:, cols] = (mixed / total).astype(jnp.bfloat16)


def attend(query, parts):
    rows, width = query.shape
    keys = sum(part.shape[1] for part in parts)
    out = jax.ShapeDtypeStruct((rows // 2, width), jnp.bfloat16)
    vmem = pl.BlockSpec(memory_space=pltpu.VMEM)
    return pl.pallas_call(
        attend_kernel,
        out_shape=(out, out),
        in_specs=[vmem] * 5,
        out_specs=(vmem, vmem),
        cost_estimate=pl.CostEstimate(
            flops=4 * rows * keys * width,
            bytes_accessed=4 * (rows + keys) * width,
            transcendentals=rows * keys * width // HEAD_SIZE,
        ),
        compiler_params=pltpu.CompilerParams(vmem_limit_bytes=32 * 1024 * 1024),
    )(query, *parts)


CHUNKS = (4, 2)


def paired_shards(latents, queries, keys, values, fresh_frames, timesteps, offsets):
    rows = latents.shape[1] * latents.shape[2]
    width = latents.shape[3]
    queries, keys, values = (a.reshape(rows, width) for a in (queries, keys, values))
    place = lax.axis_index("seq")
    jobs = []
    for bit, other, base in ((ACROSS, DOWN, 0), (DOWN, ACROSS, width // 2)):
        side = (place // bit) % 2
        start = 0
        for heads in CHUNKS:
            size = heads * HEAD_SIZE
            mine = base + side * (width // 4) + start
            theirs = base + (1 - side) * (width // 4) + start
            jobs.append((bit, other, side, size, mine, theirs))
            start += size
    jobs = [jobs[0], jobs[2], jobs[1], jobs[3]]

    def cut(array, at, size):
        return lax.dynamic_slice(array, (0, at), (rows, size))

    arrived = []
    for bit, other, side, size, mine, theirs in jobs:
        send = jnp.stack([cut(a, theirs, size) for a in (keys, values, queries)])
        arrived.append(swapped(send, bit))
    near = []
    far = []
    for (bit, other, side, size, mine, theirs), got in zip(jobs, arrived):
        own = jnp.stack([cut(a, mine, size) for a in (keys, values)])
        near.append(jnp.concatenate([own, got[:2]], axis=1))
        far.append(swapped(near[-1], other))
    halves = []
    for (bit, other, side, size, mine, theirs), got, here, there in zip(jobs, arrived, near, far):
        query = jnp.concatenate([cut(queries, mine, size), got[2]], axis=0)
        own, back = attend(query, (here, there, swapped(here, CORE), swapped(there, CORE)))
        back = swapped(back, bit)
        first = jnp.where(side == 0, own, back)
        second = jnp.where(side == 0, back, own)
        halves.append((first, second))
    order = []
    for a, b in ((0, 2), (1, 3)):
        order += [halves[a][0], halves[b][0], halves[a][1], halves[b][1]]
    attended = jnp.concatenate(order, axis=1).reshape(latents.shape)
    return (attended, advance(latents, attended, fresh_frames, timesteps, offsets))


def solution(mesh):
    in_specs = (
        P("queue", None, "seq", None),
        P("queue", None, "seq", None),
        P("queue", None, "seq", None),
        P("queue", None, "seq", None),
        P(None, "seq", None),
        P(),
        P("queue"),
    )
    out_specs = (P("queue", None, "seq", None), P("queue", None, "seq", None))
    shards = paired_shards if mesh.shape["seq"] == 8 else grouped_shards
    return jax.shard_map(shards, mesh=mesh, in_specs=in_specs, out_specs=out_specs, check_vma=False)
```

```python
import functools
import jax
import jax.numpy as jnp
from jax import lax
from jax.experimental import pallas as pl
from jax.experimental.pallas import tpu as pltpu
from jax.sharding import PartitionSpec as P

HEAD_SIZE = 128
GROUPS = 8
HEAD_GRP = 3
MAX_SHIFT = 2
LOG2E = 1.4426950408889634
CORE, ACROSS, DOWN = 1, 2, 4


def shifted(block, axis, distance):
    devices = range(lax.axis_size(axis))
    route = [(i - distance, i) for i in devices if i - distance in devices]
    return lax.ppermute(block, axis, route)


def swapped(block, bit):
    return lax.ppermute(block, "seq", [(i, i ^ bit) for i in range(lax.axis_size("seq"))])


def after(block, *others):
    return lax.optimization_barrier((block, *others))[0]


def level(step, count):
    ratio = step.astype(jnp.float32) / count
    return 7.0 * ratio / (1.0 + 6.0 * ratio)


def advance(latents, attended, fresh_frames, timesteps, offsets):
    queue_count = lax.axis_size("queue")
    position = lax.axis_index("queue")
    frame_count = latents.shape[1]
    level_count = 8 * queue_count
    own_step = lax.dynamic_index_in_dim(timesteps, position, 0, keepdims=False)
    delta = 8.0 * (level(own_step - 1, level_count) - level(own_step, level_count))
    updated = (latents.astype(jnp.float32) + delta * attended.astype(jnp.float32)).astype(
        jnp.bfloat16
    )
    incoming = shifted(updated[:, :MAX_SHIFT], "queue", -1)
    incoming = jnp.where(position == queue_count - 1, fresh_frames[None], incoming)
    joined = jnp.concatenate([updated, incoming], axis=1)
    return lax.dynamic_slice_in_dim(joined, offsets[0], frame_count, 1)


def attend_items(query_part, key_part, value_part):
    length = query_part.shape[0]
    block = min(512, length)
    scale = HEAD_SIZE ** (-0.5)
    results = []
    for item in range(query_part.shape[1]):
        key_head = key_part[:, item]
        value_head = value_part[:, item]

        def one_block(query_block):
            scores = (
                jnp.einsum("qd,kd->qk", query_block, key_head, preferred_element_type=jnp.float32)
                * scale
            )
            top = jnp.max(scores, axis=-1, keepdims=True)
            weights = jnp.exp(scores - top)
            total = jnp.sum(weights, axis=-1, keepdims=True)
            mixed = (
                jnp.dot(
                    weights.astype(jnp.bfloat16), value_head, preferred_element_type=jnp.float32
                )
                / total
            )
            return mixed.astype(jnp.bfloat16)

        blocks = query_part[:, item].reshape(length // block, block, HEAD_SIZE)
        results.append(lax.map(one_block, blocks).reshape(length, HEAD_SIZE))
    return jnp.stack(results, axis=1)


def grouped_shards(latents, queries, keys, values, fresh_frames, timesteps, offsets):
    frame_count = latents.shape[1]
    frame_rows = latents.shape[2]
    seq_count = lax.axis_size("seq")
    quarters = seq_count // GROUPS
    row_count = frame_count * frame_rows
    quarter_rows = row_count // quarters
    quarter = lax.axis_index("seq") // GROUPS
    split_keys = keys.reshape(row_count, 1, GROUPS, HEAD_GRP, 1, HEAD_SIZE)
    split_values = values.reshape(row_count, 1, GROUPS, HEAD_GRP, 1, HEAD_SIZE)
    split_queries = queries.reshape(row_count, 1, GROUPS, HEAD_GRP, 1, HEAD_SIZE)
    triple = jnp.concatenate([split_queries, split_keys, split_values], axis=4)
    triple = jnp.broadcast_to(triple, (row_count, quarters, GROUPS, HEAD_GRP, 3, HEAD_SIZE))
    triple = triple.reshape(row_count, seq_count, HEAD_GRP, 3, HEAD_SIZE)
    piece = lax.all_to_all(triple, "seq", split_axis=1, concat_axis=0, tiled=True)
    items = piece.shape[2]
    query_part = piece[:, 0, :, 0].reshape(seq_count, quarter_rows, quarters, items, HEAD_SIZE)
    query_part = lax.dynamic_index_in_dim(query_part, quarter, 2, keepdims=False)
    query_part = query_part.reshape(seq_count * quarter_rows, items, HEAD_SIZE)
    outcome = attend_items(query_part, piece[:, 0, :, 1], piece[:, 0, :, 2])
    outcome = outcome.reshape(seq_count, quarter_rows, HEAD_GRP * HEAD_SIZE)
    gathered = lax.all_to_all(outcome, "seq", split_axis=0, concat_axis=2, tiled=True)
    attended = gathered.reshape(latents.shape)
    return (attended, advance(latents, attended, fresh_frames, timesteps, offsets))


CHUNKS = (4, 2)
VMEM_LIMIT = 16 * 1024 * 1024
PACK_LIMIT = 249 * 256 * 1024
VMEM = pl.BlockSpec(memory_space=pltpu.VMEM)
SMEM = pl.BlockSpec(memory_space=pltpu.SMEM)
HBM = pl.BlockSpec(memory_space=pltpu.HBM)


def call(kernel, out_shape, in_specs, out_specs, scratch_shapes=(), cost=(0, 0, 0), **options):
    limit = options.pop("limit", VMEM_LIMIT)
    return pl.pallas_call(
        kernel,
        out_shape=out_shape,
        in_specs=in_specs,
        out_specs=out_specs,
        scratch_shapes=scratch_shapes,
        cost_estimate=pl.CostEstimate(
            flops=cost[0], bytes_accessed=cost[1], transcendentals=cost[2]
        ),
        compiler_params=pltpu.CompilerParams(vmem_limit_bytes=limit),
        **options,
    )


def half_start(side, mine, width):
    bit, _, base = side
    index = (lax.axis_index("seq") // bit) % 2
    index = index if mine else 1 - index
    return base + index * (width // 4)


def columns(start, size):
    return pl.ds(pl.multiple_of(start, HEAD_SIZE), size)


def step_size(timesteps_ref):
    position, queue_count = lax.axis_index("queue"), lax.axis_size("queue")
    step = jnp.full((1, HEAD_SIZE), timesteps_ref[position], jnp.int32)
    delta = 8.0 * (level(step - 1, 8 * queue_count) - level(step, 8 * queue_count))
    return delta[:, :1]


def pack_kernel(sides, *refs):
    arrays, outs, sems = refs[:3], refs[3:-1], refs[-1]
    width = arrays[0].shape[1]
    copies = []
    for index, (side, out) in enumerate(zip(sides, outs)):
        cols = columns(half_start(side, False, width), out.shape[2])
        for which, array in enumerate(arrays):
            copies.append(
                pltpu.make_async_copy(array.at[:, cols], out.at[which], sems.at[index, which])
            )
    for copy in copies:
        copy.start()
    for copy in copies:
        copy.wait()


def pack(sides, arrays):
    rows, width = arrays[0].shape
    out = jax.ShapeDtypeStruct((3, rows, width // 4), jnp.bfloat16)
    return call(
        functools.partial(pack_kernel, sides),
        (out,) * len(sides),
        [HBM] * 3,
        (VMEM,) * len(sides),
        [pltpu.SemaphoreType.DMA((len(sides), 3))],
        (0, 3 * rows * width * len(sides), 0),
        limit=PACK_LIMIT,
    )(*arrays)


def join_kernel(side, keys_ref, values_ref, got_ref, whole_ref, *part_refs):
    rows, width = keys_ref.shape
    cols = columns(half_start(side, True, width), width // 4)
    for which, source in enumerate((keys_ref, values_ref)):
        for first, block in ((0, source[:, cols]), (rows, got_ref[which])):
            whole_ref[which, first : first + rows] = block
            start = 0
            for part in part_refs:
                size = part.shape[2]
                part[which, first : first + rows] = block[:, start : start + size]
                start += size


def join(side, keys, values, got, sizes):
    rows, width = got.shape[1:]
    outs = tuple(
        jax.ShapeDtypeStruct((2, 2 * rows, size), jnp.bfloat16) for size in (width, *sizes)
    )
    return call(
        functools.partial(join_kernel, side),
        outs,
        [VMEM] * 3,
        (VMEM,) * len(outs),
        cost=(0, 24 * rows * width, 0),
    )(keys, values, got)


def attend_kernel(side, start, queries_ref, near_ref, got_ref, core_ref, far_ref, core_far_ref, own_ref, back_ref):
    rows, width = queries_ref.shape
    factor = LOG2E * HEAD_SIZE ** (-0.5)
    heads = own_ref.shape[1] // HEAD_SIZE
    first = half_start(side, True, width) + start

    def narrow(head):
        return slice(head * HEAD_SIZE, (head + 1) * HEAD_SIZE)

    def wide(head):
        return slice(start + head * HEAD_SIZE, start + (head + 1) * HEAD_SIZE)

    def tokens(which, head):
        return (
            near_ref[which, :, wide(head)],
            core_ref[which, :, wide(head)],
            far_ref[which, :, narrow(head)],
            core_far_ref[which, :, narrow(head)],
        )

    def score(head):
        query = jnp.concatenate(
            [queries_ref[:, columns(first + head * HEAD_SIZE, HEAD_SIZE)], got_ref[2, :, wide(head)]]
        )
        return [
            lax.dot_general(
                query, key, (((1,), (1,)), ((), ())), preferred_element_type=jnp.float32
            )
            for key in tokens(0, head)
        ]

    scores = score(0)
    for head in range(heads):
        following = score(head + 1) if head + 1 < heads else None
        top = jnp.maximum(jnp.maximum(scores[0], scores[1]), jnp.maximum(scores[2], scores[3]))
        top = jnp.max(top, axis=-1, keepdims=True)
        weights = [jnp.exp2((part - top) * factor) for part in scores]
        total = (weights[0] + weights[1]) + (weights[2] + weights[3])
        total = jnp.sum(total, axis=-1, keepdims=True)
        mixed = sum(
            jnp.dot(weight.astype(jnp.bfloat16), value, preferred_element_type=jnp.float32)
            for weight, value in zip(weights, tokens(1, head))
        )
        mixed = (mixed / total).astype(jnp.bfloat16)
        own_ref[:, narrow(head)] = mixed[:rows]
        back_ref[:, narrow(head)] = mixed[rows:]
        scores = following


def attend(side, start, queries, near, got, core, far, core_far):
    rows = queries.shape[0]
    keys, width = 4 * far.shape[1], far.shape[2]
    out = jax.ShapeDtypeStruct((rows, width), jnp.bfloat16)
    return call(
        functools.partial(attend_kernel, side, start),
        (out, out),
        [VMEM] * 6,
        (VMEM, VMEM),
        cost=(8 * rows * keys * width, 8 * keys * width, 2 * rows * keys * width // HEAD_SIZE),
    )(queries, near, got, core, far, core_far)


def moved(latents, attended, delta):
    change = delta * attended.astype(jnp.float32)
    return (latents.astype(jnp.float32) + change).astype(jnp.bfloat16)


def lead_kernel(places, timesteps_ref, latents_ref, *refs):
    pieces, out_ref = refs[:-1], refs[-1]
    rows, width = out_ref.shape[0], latents_ref.shape[1]
    delta = step_size(timesteps_ref)
    at = 0
    for (side, mine, start), piece in zip(places, pieces):
        size = piece.shape[1]
        cols = columns(half_start(side, mine, width) + start, size)
        out_ref[:, at : at + size] = moved(latents_ref[:rows, cols], piece[:rows], delta)
        at += size


def lead(places, rows, timesteps, latents, pieces):
    size = sum(piece.shape[1] for piece in pieces)
    return call(
        functools.partial(lead_kernel, places),
        jax.ShapeDtypeStruct((rows, size), jnp.bfloat16),
        [SMEM] + [VMEM] * (1 + len(pieces)),
        VMEM,
        cost=(2 * rows * size, 6 * rows * size, 0),
    )(timesteps, latents, *pieces)


def finish_kernel(places, timesteps_ref, offset_ref, latents_ref, *refs):
    pieces = refs[: len(places)]
    attended_ref, advanced_ref, whole_ref, updated_ref, out_sem, move_sem = refs[len(places) :]
    offset, delta = offset_ref[0], step_size(timesteps_ref)
    frames, rows, width = attended_ref.shape
    out_copies, move_copies = [], []
    for frame in range(frames):
        span = slice(frame * rows, (frame + 1) * rows)
        for (side, mine, start), piece in zip(places, pieces):
            cols = columns(half_start(side, mine, width) + start, piece.shape[1])
            whole_ref[frame, :, cols] = piece[span]
        out_copies.append(
            pltpu.make_async_copy(whole_ref.at[frame], attended_ref.at[frame], out_sem.at[frame])
        )
        out_copies[-1].start()
        if frame == 0:
            continue
        updated_ref[frame] = moved(latents_ref[span], whole_ref[frame], delta)
        copy = pltpu.make_async_copy(
            updated_ref.at[frame],
            advanced_ref.at[jnp.maximum(frame - offset, 0)],
            move_sem.at[frame],
        )
        if frame < MAX_SHIFT:
            pl.when(frame >= offset)(copy.start)
        else:
            copy.start()
        move_copies.append((frame, copy))
    for copy in out_copies:
        copy.wait()
    for frame, copy in move_copies:
        if frame < MAX_SHIFT:
            pl.when(frame >= offset)(copy.wait)
        else:
            copy.wait()


def finish(shape, places, timesteps, offsets, latents, pieces):
    out = jax.ShapeDtypeStruct(shape, jnp.bfloat16)
    return call(
        functools.partial(finish_kernel, places),
        (out, out),
        [SMEM] * 2 + [VMEM] * (1 + len(pieces)),
        (HBM, HBM),
        [
            pltpu.VMEM(shape, jnp.bfloat16),
            pltpu.VMEM(shape, jnp.bfloat16),
            pltpu.SemaphoreType.DMA((shape[0],)),
            pltpu.SemaphoreType.DMA((shape[0],)),
        ],
        (2 * latents.size, 8 * latents.size, 0),
    )(timesteps, offsets, latents, *pieces)


def fill_kernel(groups, offset_ref, fresh_ref, *refs):
    leads = refs[: len(groups)]
    _, advanced_ref, coming_ref, sem = refs[len(groups) :]
    offset = offset_ref[0]
    frames, rows, width = advanced_ref.shape
    newest = lax.axis_index("queue") == lax.axis_size("queue") - 1

    @pl.when(newest)
    def _():
        coming_ref[...] = fresh_ref[...]

    @pl.when(jnp.logical_not(newest))
    def _():
        for places, part in zip(groups, leads):
            at = 0
            for side, mine, start, size in places:
                cols = columns(half_start(side, mine, width) + start, size)
                for frame in range(MAX_SHIFT):
                    span = slice(frame * rows, (frame + 1) * rows)
                    coming_ref[frame, :, cols] = part[span, at : at + size]
                at += size

    copies = [
        pltpu.make_async_copy(
            coming_ref.at[frame],
            advanced_ref.at[jnp.minimum(frames - offset + frame, frames - 1)],
            sem.at[frame],
        )
        for frame in range(MAX_SHIFT)
    ]
    for frame, copy in enumerate(copies):
        pl.when(frame < offset)(copy.start)
    for frame, copy in enumerate(copies):
        pl.when(frame < offset)(copy.wait)


def fill(groups, offsets, fresh, leads, advanced):
    return call(
        functools.partial(fill_kernel, groups),
        jax.ShapeDtypeStruct(advanced.shape, advanced.dtype),
        [SMEM] + [VMEM] * (1 + len(leads)) + [HBM],
        HBM,
        [pltpu.VMEM(fresh.shape, jnp.bfloat16), pltpu.SemaphoreType.DMA((MAX_SHIFT,))],
        (0, 6 * fresh.size, 0),
        input_output_aliases={2 + len(leads): 0},
    )(offsets, fresh, *leads, advanced)


def paired_shards(latents, queries, keys, values, fresh_frames, timesteps, offsets):
    shape = latents.shape[1:]
    rows = shape[0] * shape[1]
    first_rows = MAX_SHIFT * shape[1]
    width = shape[2]
    latents, queries, keys, values = (
        a.reshape(rows, width) for a in (latents, queries, keys, values)
    )
    sides = ((ACROSS, DOWN, 0), (DOWN, ACROSS, width // 2))
    sizes = [heads * HEAD_SIZE for heads in CHUNKS]
    sends = pack(sides, (keys, values, queries))
    arrived = [swapped(send, side[0]) for send, side in zip(sends, sides)]
    joined = [join(side, keys, values, got, sizes) for side, got in zip(sides, arrived)]
    across = [swapped(parts[0], CORE) for parts in joined]
    pieces, places, groups, leads, outcome = [], [], [], [], []
    start = 0
    for chunk, size in enumerate(sizes):
        part_pieces, part_places = [], []
        for which, side in enumerate(sides):
            far = swapped(joined[which][1 + chunk], side[1])
            if chunk:
                far = after(far, outcome[-len(sides)])
            own, back = attend(
                side,
                start,
                queries,
                joined[which][0],
                arrived[which],
                across[which],
                far,
                swapped(far, CORE),
            )
            outcome.append(own)
            part_pieces += [own, swapped(back, side[0])]
            part_places += [(side, True, start), (side, False, start)]
        head = lead(part_places, first_rows, timesteps, latents, part_pieces)
        leads.append(shifted(head, "queue", -1))
        groups.append([(*place, size) for place in part_places])
        pieces += part_pieces
        places += part_places
        start += size
    attended, advanced = finish(shape, places, timesteps, offsets, latents, pieces)
    advanced = fill(groups, offsets, fresh_frames, leads, advanced)
    return (attended[None], advanced[None])


def solution(mesh):
    in_specs = (
        P("queue", None, "seq", None),
        P("queue", None, "seq", None),
        P("queue", None, "seq", None),
        P("queue", None, "seq", None),
        P(None, "seq", None),
        P(),
        P("queue"),
    )
    out_specs = (P("queue", None, "seq", None), P("queue", None, "seq", None))
    shards = paired_shards if mesh.shape["seq"] == 8 else grouped_shards
    return jax.shard_map(shards, mesh=mesh, in_specs=in_specs, out_specs=out_specs, check_vma=False)
```

```python
import functools
import jax
import jax.numpy as jnp
from jax import lax
from jax.experimental import pallas as pl
from jax.experimental.pallas import tpu as pltpu
from jax.sharding import PartitionSpec as P

HEAD_SIZE = 128
GROUPS = 8
HEAD_GRP = 3
MAX_SHIFT = 2
LOG2E = 1.4426950408889634
CORE, ACROSS, DOWN = 1, 2, 4


def shifted(block, axis, distance):
    devices = range(lax.axis_size(axis))
    route = [(i - distance, i) for i in devices if i - distance in devices]
    return lax.ppermute(block, axis, route)


def swapped(block, bit):
    return lax.ppermute(block, "seq", [(i, i ^ bit) for i in range(lax.axis_size("seq"))])


def after(block, *others):
    return lax.optimization_barrier((block, *others))[0]


def level(step, count):
    ratio = step.astype(jnp.float32) / count
    return 7.0 * ratio / (1.0 + 6.0 * ratio)


def advance(latents, attended, fresh_frames, timesteps, offsets):
    queue_count = lax.axis_size("queue")
    position = lax.axis_index("queue")
    frame_count = latents.shape[1]
    level_count = 8 * queue_count
    own_step = lax.dynamic_index_in_dim(timesteps, position, 0, keepdims=False)
    delta = 8.0 * (level(own_step - 1, level_count) - level(own_step, level_count))
    updated = (latents.astype(jnp.float32) + delta * attended.astype(jnp.float32)).astype(
        jnp.bfloat16
    )
    incoming = shifted(updated[:, :MAX_SHIFT], "queue", -1)
    incoming = jnp.where(position == queue_count - 1, fresh_frames[None], incoming)
    joined = jnp.concatenate([updated, incoming], axis=1)
    return lax.dynamic_slice_in_dim(joined, offsets[0], frame_count, 1)


def attend_items(query_part, key_part, value_part):
    length = query_part.shape[0]
    block = min(512, length)
    scale = HEAD_SIZE ** (-0.5)
    results = []
    for item in range(query_part.shape[1]):
        key_head = key_part[:, item]
        value_head = value_part[:, item]

        def one_block(query_block):
            scores = (
                jnp.einsum("qd,kd->qk", query_block, key_head, preferred_element_type=jnp.float32)
                * scale
            )
            top = jnp.max(scores, axis=-1, keepdims=True)
            weights = jnp.exp(scores - top)
            total = jnp.sum(weights, axis=-1, keepdims=True)
            mixed = (
                jnp.dot(
                    weights.astype(jnp.bfloat16), value_head, preferred_element_type=jnp.float32
                )
                / total
            )
            return mixed.astype(jnp.bfloat16)

        blocks = query_part[:, item].reshape(length // block, block, HEAD_SIZE)
        results.append(lax.map(one_block, blocks).reshape(length, HEAD_SIZE))
    return jnp.stack(results, axis=1)


def grouped_shards(latents, queries, keys, values, fresh_frames, timesteps, offsets):
    frame_count = latents.shape[1]
    frame_rows = latents.shape[2]
    seq_count = lax.axis_size("seq")
    quarters = seq_count // GROUPS
    row_count = frame_count * frame_rows
    quarter_rows = row_count // quarters
    quarter = lax.axis_index("seq") // GROUPS
    split_keys = keys.reshape(row_count, 1, GROUPS, HEAD_GRP, 1, HEAD_SIZE)
    split_values = values.reshape(row_count, 1, GROUPS, HEAD_GRP, 1, HEAD_SIZE)
    split_queries = queries.reshape(row_count, 1, GROUPS, HEAD_GRP, 1, HEAD_SIZE)
    triple = jnp.concatenate([split_queries, split_keys, split_values], axis=4)
    triple = jnp.broadcast_to(triple, (row_count, quarters, GROUPS, HEAD_GRP, 3, HEAD_SIZE))
    triple = triple.reshape(row_count, seq_count, HEAD_GRP, 3, HEAD_SIZE)
    piece = lax.all_to_all(triple, "seq", split_axis=1, concat_axis=0, tiled=True)
    items = piece.shape[2]
    query_part = piece[:, 0, :, 0].reshape(seq_count, quarter_rows, quarters, items, HEAD_SIZE)
    query_part = lax.dynamic_index_in_dim(query_part, quarter, 2, keepdims=False)
    query_part = query_part.reshape(seq_count * quarter_rows, items, HEAD_SIZE)
    outcome = attend_items(query_part, piece[:, 0, :, 1], piece[:, 0, :, 2])
    outcome = outcome.reshape(seq_count, quarter_rows, HEAD_GRP * HEAD_SIZE)
    gathered = lax.all_to_all(outcome, "seq", split_axis=0, concat_axis=2, tiled=True)
    attended = gathered.reshape(latents.shape)
    return (attended, advance(latents, attended, fresh_frames, timesteps, offsets))


VMEM_LIMIT = 16 * 1024 * 1024
PACK_LIMIT = 249 * 256 * 1024
VMEM = pl.BlockSpec(memory_space=pltpu.VMEM)
SMEM = pl.BlockSpec(memory_space=pltpu.SMEM)
HBM = pl.BlockSpec(memory_space=pltpu.HBM)


def call(kernel, out_shape, in_specs, out_specs, scratch_shapes=(), cost=(0, 0, 0), **options):
    limit = options.pop("limit", VMEM_LIMIT)
    return pl.pallas_call(
        kernel,
        out_shape=out_shape,
        in_specs=in_specs,
        out_specs=out_specs,
        scratch_shapes=scratch_shapes,
        cost_estimate=pl.CostEstimate(
            flops=cost[0], bytes_accessed=cost[1], transcendentals=cost[2]
        ),
        compiler_params=pltpu.CompilerParams(vmem_limit_bytes=limit),
        **options,
    )


def columns(side, mask, width):
    bit, _, base = side
    index = lax.bitwise_xor(lax.axis_index("seq"), mask)
    start = base + (index // bit) % 2 * (width // 4) + index % 2 * (width // 8)
    return pl.ds(pl.multiple_of(start, HEAD_SIZE), width // 8)


def half_columns(side, mask, width):
    bit, _, base = side
    index = lax.bitwise_xor(lax.axis_index("seq"), mask)
    start = base + (index // bit) % 2 * (width // 4)
    return pl.ds(pl.multiple_of(start, HEAD_SIZE), width // 4)


def share(other, width, skip=0, size=None):
    index = (lax.axis_index("seq") + other) % 2
    return pl.ds(pl.multiple_of(index * (width // 2) + skip, HEAD_SIZE), size or width // 2)


def peers(side):
    return (CORE, side[0], side[0] | CORE)


def step_size(timesteps_ref):
    position, queue_count = lax.axis_index("queue"), lax.axis_size("queue")
    step = jnp.full((1, HEAD_SIZE), timesteps_ref[position], jnp.int32)
    delta = 8.0 * (level(step - 1, 8 * queue_count) - level(step, 8 * queue_count))
    return delta[:, :1]


def pack_kernel(cuts, *refs):
    arrays, outs, sems = refs[:3], refs[3:-1], refs[-1]
    width = arrays[0].shape[1]
    copies = []
    for index, ((cut, side, mask, _), out) in enumerate(zip(cuts, outs)):
        for which in range(out.shape[0]):
            source = arrays[which].at[:, cut(side, mask, width)]
            copies.append(pltpu.make_async_copy(source, out.at[which], sems.at[index, which]))
    for copy in copies:
        copy.start()
    for copy in copies:
        copy.wait()


def pack(cuts, arrays, limit):
    rows, width = arrays[0].shape
    outs = tuple(
        jax.ShapeDtypeStruct(
            (count, rows, width // (4 if cut is half_columns else 8)), jnp.bfloat16
        )
        for cut, _, _, count in cuts
    )
    return call(
        functools.partial(pack_kernel, cuts),
        outs,
        [HBM] * 3,
        (VMEM,) * len(outs),
        [pltpu.SemaphoreType.DMA((len(outs), 3))],
        (0, sum(4 * out.size for out in outs), 0),
        limit=limit,
    )(*arrays)


def split_kernel(got_ref, out_ref):
    out_ref[...] = got_ref[:, :, share(1, got_ref.shape[2])]


def split(got):
    count, rows, width = got.shape
    return call(
        split_kernel,
        jax.ShapeDtypeStruct((count, rows, width // 2), jnp.bfloat16),
        [VMEM],
        VMEM,
        cost=(0, 2 * got.size, 0),
    )(got)


def join_kernel(got_ref, core_ref, out_ref):
    rows = got_ref.shape[1]
    for which in range(2):
        out_ref[which, :rows] = got_ref[which, :, share(0, got_ref.shape[2])]
        out_ref[which, rows:] = core_ref[which]


def join(got, core):
    rows, size = core.shape[1:]
    return call(
        join_kernel,
        jax.ShapeDtypeStruct((2, 2 * rows, size), jnp.bfloat16),
        [VMEM] * 2,
        VMEM,
        cost=(0, 16 * rows * size, 0),
    )(got, core)


def weigh(scores, values, before=None):
    factor = LOG2E * HEAD_SIZE ** (-0.5)
    shape = (scores[0].shape[0], HEAD_SIZE)
    top = jnp.max(functools.reduce(jnp.maximum, scores), axis=-1, keepdims=True)
    top = jnp.broadcast_to(top, shape)
    if before is not None:
        top = jnp.maximum(top, before[1])
    tops = jnp.concatenate([top] * (scores[0].shape[1] // HEAD_SIZE), axis=1)
    weights = [jnp.exp2((part - tops) * factor) for part in scores]
    total = jnp.sum(functools.reduce(jnp.add, weights), axis=-1, keepdims=True)
    total = jnp.broadcast_to(total, shape)
    mixed = sum(
        jnp.dot(weight.astype(jnp.bfloat16), value, preferred_element_type=jnp.float32)
        for weight, value in zip(weights, values)
    )
    if before is not None:
        keep = jnp.exp2((before[1] - top) * factor)
        mixed = mixed + keep * before[0]
        total = total + keep * before[2]
    return mixed, top, total


def dots(query, keys):
    return [
        lax.dot_general(query, key, (((1,), (1,)), ((), ())), preferred_element_type=jnp.float32)
        for key in keys
    ]


def attend_kernel(
    side,
    keys_ref,
    values_ref,
    queries_ref,
    core_ref,
    got_ref,
    got_core_ref,
    far_ref,
    far_core_ref,
    *outs,
):
    rows, width = queries_ref.shape
    wholes = (keys_ref, values_ref, queries_ref)
    first = columns(side, 0, width).start
    tasks = [(head, pair) for head in range(core_ref.shape[2] // HEAD_SIZE) for pair in range(2)]

    def tokens(which, head):
        start = head * HEAD_SIZE
        cols = slice(start, start + HEAD_SIZE)
        mine = pl.ds(pl.multiple_of(first + start, HEAD_SIZE), HEAD_SIZE)
        ours = share(0, got_ref.shape[2], start, HEAD_SIZE)
        parts = [
            (wholes[which][:, mine], core_ref[which, :, cols]),
            (got_ref[which, :, ours], got_core_ref[which, :, cols]),
        ]
        if which < 2:
            parts.append((far_ref[which, :, ours], far_core_ref[which, :, cols]))
        return [jnp.concatenate(part) for part in parts]

    def score(head, pair):
        return dots(tokens(2, head)[pair], tokens(0, head))

    scores = score(*tasks[0])
    for index, (head, pair) in enumerate(tasks):
        following = score(*tasks[index + 1]) if index + 1 < len(tasks) else None
        cols = slice(head * HEAD_SIZE, (head + 1) * HEAD_SIZE)
        for out, value in zip(outs, weigh(scores, tokens(1, head))):
            out[2 * rows * pair : 2 * rows * (pair + 1), cols] = value
        scores = following


def attend(side, *arrays):
    rows, width = arrays[0].shape
    size = width // 8
    out = jax.ShapeDtypeStruct((4 * rows, size), jnp.float32)
    return call(
        functools.partial(attend_kernel, side),
        (out,) * 3,
        [VMEM] * 8,
        (VMEM,) * 3,
        cost=(96 * rows * rows * size, 64 * rows * size, 24 * rows * rows * size // HEAD_SIZE),
    )(*arrays)


def complete_kernel(side, queries_ref, core_ref, got_ref, got_core_ref, far_got_ref, *refs):
    old, outs = refs[:3], refs[3:]
    rows, width = queries_ref.shape
    first = columns(side, 0, width).start
    tasks = [(head, pair) for head in range(core_ref.shape[2] // HEAD_SIZE) for pair in range(2)]

    def score(head, pair):
        start = head * HEAD_SIZE
        cols = slice(start, start + HEAD_SIZE)
        if pair == 0:
            mine = pl.ds(pl.multiple_of(first + start, HEAD_SIZE), HEAD_SIZE)
            query = (queries_ref[:, mine], core_ref[2, :, cols])
        else:
            ours = share(0, got_ref.shape[2], start, HEAD_SIZE)
            query = (got_ref[2, :, ours], got_core_ref[2, :, cols])
        return dots(jnp.concatenate(query), [far_got_ref[0, :, cols]])

    scores = score(*tasks[0])
    for index, (head, pair) in enumerate(tasks):
        following = score(*tasks[index + 1]) if index + 1 < len(tasks) else None
        cols = slice(head * HEAD_SIZE, (head + 1) * HEAD_SIZE)
        before = [ref[2 * rows * pair : 2 * rows * (pair + 1), cols] for ref in old]
        mixed, _, total = weigh(scores, [far_got_ref[1, :, cols]], before)
        mixed = (mixed / total).astype(jnp.bfloat16)
        outs[2 * pair][:, cols] = mixed[:rows]
        outs[2 * pair + 1][:, cols] = mixed[rows:]
        scores = following


def complete(side, queries, core, got, far_core, far_got, old):
    rows, width = queries.shape
    size = width // 8
    out = jax.ShapeDtypeStruct((rows, size), jnp.bfloat16)
    return call(
        functools.partial(complete_kernel, side),
        (out,) * 4,
        [VMEM] * 8,
        (VMEM,) * 4,
        cost=(32 * rows * rows * size, 64 * rows * size, 8 * rows * rows * size // HEAD_SIZE),
    )(queries, core, got, far_core, far_got, *old)


def moved(latents, attended, delta):
    change = delta * attended.astype(jnp.float32)
    return (latents.astype(jnp.float32) + change).astype(jnp.bfloat16)


def lead_kernel(places, timesteps_ref, latents_ref, *refs):
    pieces, out_ref = refs[:-1], refs[-1]
    rows, width = out_ref.shape[0], latents_ref.shape[1]
    delta = step_size(timesteps_ref)
    at = 0
    for place, piece in zip(places, pieces):
        size = piece.shape[1]
        cols = columns(*place, width)
        out_ref[:, at : at + size] = moved(latents_ref[:rows, cols], piece[:rows], delta)
        at += size


def lead(places, rows, timesteps, latents, pieces):
    size = sum(piece.shape[1] for piece in pieces)
    return call(
        functools.partial(lead_kernel, places),
        jax.ShapeDtypeStruct((rows, size), jnp.bfloat16),
        [SMEM] + [VMEM] * (1 + len(pieces)),
        VMEM,
        cost=(2 * rows * size, 6 * rows * size, 0),
    )(timesteps, latents, *pieces)


def finish_kernel(places, timesteps_ref, offset_ref, latents_ref, *refs):
    pieces = refs[: len(places)]
    attended_ref, advanced_ref, whole_ref, updated_ref, out_sem, move_sem = refs[len(places) :]
    offset, delta = offset_ref[0], step_size(timesteps_ref)
    frames, rows, width = attended_ref.shape
    out_copies, move_copies = [], []
    for frame in range(frames):
        span = slice(frame * rows, (frame + 1) * rows)
        for place, piece in zip(places, pieces):
            cols = columns(*place, width)
            whole_ref[frame, :, cols] = piece[span]
        out_copies.append(
            pltpu.make_async_copy(whole_ref.at[frame], attended_ref.at[frame], out_sem.at[frame])
        )
        out_copies[-1].start()
        if frame == 0:
            continue
        updated_ref[frame] = moved(latents_ref[span], whole_ref[frame], delta)
        copy = pltpu.make_async_copy(
            updated_ref.at[frame],
            advanced_ref.at[jnp.maximum(frame - offset, 0)],
            move_sem.at[frame],
        )
        if frame < MAX_SHIFT:
            pl.when(frame >= offset)(copy.start)
        else:
            copy.start()
        move_copies.append((frame, copy))
    for copy in out_copies:
        copy.wait()
    for frame, copy in move_copies:
        if frame < MAX_SHIFT:
            pl.when(frame >= offset)(copy.wait)
        else:
            copy.wait()


def finish(shape, places, timesteps, offsets, latents, pieces):
    out = jax.ShapeDtypeStruct(shape, jnp.bfloat16)
    return call(
        functools.partial(finish_kernel, places),
        (out, out),
        [SMEM] * 2 + [VMEM] * (1 + len(pieces)),
        (HBM, HBM),
        [
            pltpu.VMEM(shape, jnp.bfloat16),
            pltpu.VMEM(shape, jnp.bfloat16),
            pltpu.SemaphoreType.DMA((shape[0],)),
            pltpu.SemaphoreType.DMA((shape[0],)),
        ],
        (2 * latents.size, 8 * latents.size, 0),
    )(timesteps, offsets, latents, *pieces)


def fill_kernel(groups, offset_ref, fresh_ref, *refs):
    leads = refs[: len(groups)]
    _, advanced_ref, coming_ref, sem = refs[len(groups) :]
    offset = offset_ref[0]
    frames, rows, width = advanced_ref.shape
    newest = lax.axis_index("queue") == lax.axis_size("queue") - 1

    @pl.when(newest)
    def _():
        coming_ref[...] = fresh_ref[...]

    @pl.when(jnp.logical_not(newest))
    def _():
        for places, part in zip(groups, leads):
            at = 0
            size = part.shape[1] // len(places)
            for place in places:
                cols = columns(*place, width)
                for frame in range(MAX_SHIFT):
                    span = slice(frame * rows, (frame + 1) * rows)
                    coming_ref[frame, :, cols] = part[span, at : at + size]
                at += size

    copies = [
        pltpu.make_async_copy(
            coming_ref.at[frame],
            advanced_ref.at[jnp.minimum(frames - offset + frame, frames - 1)],
            sem.at[frame],
        )
        for frame in range(MAX_SHIFT)
    ]
    for frame, copy in enumerate(copies):
        pl.when(frame < offset)(copy.start)
    for frame, copy in enumerate(copies):
        pl.when(frame < offset)(copy.wait)


def fill(groups, offsets, fresh, leads, advanced):
    return call(
        functools.partial(fill_kernel, groups),
        jax.ShapeDtypeStruct(advanced.shape, advanced.dtype),
        [SMEM] + [VMEM] * (1 + len(leads)) + [HBM],
        HBM,
        [pltpu.VMEM(fresh.shape, jnp.bfloat16), pltpu.SemaphoreType.DMA((MAX_SHIFT,))],
        (0, 6 * fresh.size, 0),
        input_output_aliases={2 + len(leads): 0},
    )(offsets, fresh, *leads, advanced)


def paired_shards(latents, queries, keys, values, fresh_frames, timesteps, offsets):
    shape = latents.shape[1:]
    rows = shape[0] * shape[1]
    first_rows = MAX_SHIFT * shape[1]
    width = shape[2]
    latents, queries, keys, values = (
        a.reshape(rows, width) for a in (latents, queries, keys, values)
    )
    sides = ((ACROSS, DOWN, 0), (DOWN, ACROSS, width // 2))
    arrays = (keys, values, queries)
    sends = pack([(half_columns, side, side[0], 3) for side in sides], arrays, PACK_LIMIT)
    owns = pack([(half_columns, side, 0, 2) for side in sides], arrays, VMEM_LIMIT)
    cores = pack([(columns, side, CORE, 3) for side in sides], arrays, VMEM_LIMIT)
    gots = [swapped(send, side[0]) for side, send in zip(sides, sends)]
    fars = [swapped(own, side[1]) for side, own in zip(sides, owns)]
    cores = [swapped(core, CORE) for core in cores]
    far_cores = [swapped(split(far), CORE) for far in fars]
    got_cores = [swapped(split(got), CORE) for got in gots]
    far_gots = [
        swapped(join(got, core), side[1]) for side, got, core in zip(sides, gots, got_cores)
    ]
    received = list(zip(cores, gots, got_cores, fars, far_cores))
    states = [attend(side, *arrays, *parts) for side, parts in zip(sides, received)]
    far_gots = [after(far, states[1 - index][0]) for index, far in enumerate(far_gots)]
    pieces, places, groups, leads = [], [], [], []
    for index, side in enumerate(sides):
        own, *backs = complete(
            side,
            queries,
            cores[index],
            gots[index],
            got_cores[index],
            far_gots[index],
            states[index],
        )
        groups.append([(side, mask) for mask in (0, *peers(side))])
        parts = [own] + [swapped(back, mask) for back, mask in zip(backs, peers(side))]
        head = lead(groups[-1], first_rows, timesteps, latents, parts)
        leads.append(shifted(head, "queue", -1))
        pieces += parts
        places += groups[-1]
    attended, advanced = finish(shape, places, timesteps, offsets, latents, pieces)
    advanced = fill(groups, offsets, fresh_frames, leads, advanced)
    return (attended[None], advanced[None])


def solution(mesh):
    in_specs = (
        P("queue", None, "seq", None),
        P("queue", None, "seq", None),
        P("queue", None, "seq", None),
        P("queue", None, "seq", None),
        P(None, "seq", None),
        P(),
        P("queue"),
    )
    out_specs = (P("queue", None, "seq", None), P("queue", None, "seq", None))
    shards = paired_shards if mesh.shape["seq"] == 8 else grouped_shards
    return jax.shard_map(shards, mesh=mesh, in_specs=in_specs, out_specs=out_specs, check_vma=False)
```

```python
import functools
import jax
import jax.numpy as jnp
from jax import lax
from jax.experimental import pallas as pl
from jax.experimental.pallas import tpu as pltpu
from jax.sharding import PartitionSpec as P

HEAD_SIZE = 128
GROUPS = 8
HEAD_GRP = 3
MAX_SHIFT = 2
LOG2E = 1.4426950408889634
CORE, ACROSS, DOWN = 1, 2, 4


def shifted(block, axis, distance):
    devices = range(lax.axis_size(axis))
    route = [(i - distance, i) for i in devices if i - distance in devices]
    return lax.ppermute(block, axis, route)


def swapped(block, bit):
    return lax.ppermute(block, "seq", [(i, i ^ bit) for i in range(lax.axis_size("seq"))])


def after(block, *others):
    return lax.optimization_barrier((block, *others))[0]


def level(step, count):
    ratio = step.astype(jnp.float32) / count
    return 7.0 * ratio / (1.0 + 6.0 * ratio)


def advance(latents, attended, fresh_frames, timesteps, offsets):
    queue_count = lax.axis_size("queue")
    position = lax.axis_index("queue")
    frame_count = latents.shape[1]
    level_count = 8 * queue_count
    own_step = lax.dynamic_index_in_dim(timesteps, position, 0, keepdims=False)
    delta = 8.0 * (level(own_step - 1, level_count) - level(own_step, level_count))
    updated = (latents.astype(jnp.float32) + delta * attended.astype(jnp.float32)).astype(
        jnp.bfloat16
    )
    incoming = shifted(updated[:, :MAX_SHIFT], "queue", -1)
    incoming = jnp.where(position == queue_count - 1, fresh_frames[None], incoming)
    joined = jnp.concatenate([updated, incoming], axis=1)
    return lax.dynamic_slice_in_dim(joined, offsets[0], frame_count, 1)


def attend_items(query_part, key_part, value_part):
    length = query_part.shape[0]
    block = min(512, length)
    scale = HEAD_SIZE ** (-0.5)
    results = []
    for item in range(query_part.shape[1]):
        key_head = key_part[:, item]
        value_head = value_part[:, item]

        def one_block(query_block):
            scores = (
                jnp.einsum("qd,kd->qk", query_block, key_head, preferred_element_type=jnp.float32)
                * scale
            )
            top = jnp.max(scores, axis=-1, keepdims=True)
            weights = jnp.exp(scores - top)
            total = jnp.sum(weights, axis=-1, keepdims=True)
            mixed = (
                jnp.dot(
                    weights.astype(jnp.bfloat16), value_head, preferred_element_type=jnp.float32
                )
                / total
            )
            return mixed.astype(jnp.bfloat16)

        blocks = query_part[:, item].reshape(length // block, block, HEAD_SIZE)
        results.append(lax.map(one_block, blocks).reshape(length, HEAD_SIZE))
    return jnp.stack(results, axis=1)


def grouped_shards(latents, queries, keys, values, fresh_frames, timesteps, offsets):
    frame_count = latents.shape[1]
    frame_rows = latents.shape[2]
    seq_count = lax.axis_size("seq")
    quarters = seq_count // GROUPS
    row_count = frame_count * frame_rows
    quarter_rows = row_count // quarters
    quarter = lax.axis_index("seq") // GROUPS
    split_keys = keys.reshape(row_count, 1, GROUPS, HEAD_GRP, 1, HEAD_SIZE)
    split_values = values.reshape(row_count, 1, GROUPS, HEAD_GRP, 1, HEAD_SIZE)
    split_queries = queries.reshape(row_count, 1, GROUPS, HEAD_GRP, 1, HEAD_SIZE)
    triple = jnp.concatenate([split_queries, split_keys, split_values], axis=4)
    triple = jnp.broadcast_to(triple, (row_count, quarters, GROUPS, HEAD_GRP, 3, HEAD_SIZE))
    triple = triple.reshape(row_count, seq_count, HEAD_GRP, 3, HEAD_SIZE)
    piece = lax.all_to_all(triple, "seq", split_axis=1, concat_axis=0, tiled=True)
    items = piece.shape[2]
    query_part = piece[:, 0, :, 0].reshape(seq_count, quarter_rows, quarters, items, HEAD_SIZE)
    query_part = lax.dynamic_index_in_dim(query_part, quarter, 2, keepdims=False)
    query_part = query_part.reshape(seq_count * quarter_rows, items, HEAD_SIZE)
    outcome = attend_items(query_part, piece[:, 0, :, 1], piece[:, 0, :, 2])
    outcome = outcome.reshape(seq_count, quarter_rows, HEAD_GRP * HEAD_SIZE)
    gathered = lax.all_to_all(outcome, "seq", split_axis=0, concat_axis=2, tiled=True)
    attended = gathered.reshape(latents.shape)
    return (attended, advance(latents, attended, fresh_frames, timesteps, offsets))


VMEM_LIMIT = 16 * 1024 * 1024
VMEM = pl.BlockSpec(memory_space=pltpu.VMEM)
SMEM = pl.BlockSpec(memory_space=pltpu.SMEM)
HBM = pl.BlockSpec(memory_space=pltpu.HBM)


def call(kernel, out_shape, in_specs, out_specs, scratch_shapes=(), cost=(0, 0, 0), **options):
    return pl.pallas_call(
        kernel,
        out_shape=out_shape,
        in_specs=in_specs,
        out_specs=out_specs,
        scratch_shapes=scratch_shapes,
        cost_estimate=pl.CostEstimate(
            flops=cost[0], bytes_accessed=cost[1], transcendentals=cost[2]
        ),
        compiler_params=pltpu.CompilerParams(vmem_limit_bytes=VMEM_LIMIT),
        **options,
    )


def columns(side, mask, width):
    bit, _, base = side
    index = lax.bitwise_xor(lax.axis_index("seq"), mask)
    start = base + (index // bit) % 2 * (width // 4) + index % 2 * (width // 8)
    return pl.ds(pl.multiple_of(start, HEAD_SIZE), width // 8)


def half_columns(side, mask, width):
    bit, _, base = side
    index = lax.bitwise_xor(lax.axis_index("seq"), mask)
    start = base + (index // bit) % 2 * (width // 4)
    return pl.ds(pl.multiple_of(start, HEAD_SIZE), width // 4)


def share(other, width, skip=0, size=None):
    index = (lax.axis_index("seq") + other) % 2
    return pl.ds(pl.multiple_of(index * (width // 2) + skip, HEAD_SIZE), size or width // 2)


def peers(side):
    return (CORE, side[0], side[0] | CORE)


def step_kernel(timesteps_ref, out_ref):
    position, queue_count = lax.axis_index("queue"), lax.axis_size("queue")
    step = jnp.full(out_ref.shape, timesteps_ref[position], jnp.int32)
    out_ref[...] = 8.0 * (level(step - 1, 8 * queue_count) - level(step, 8 * queue_count))


def step_size(timesteps):
    out = jax.ShapeDtypeStruct((1, HEAD_SIZE), jnp.float32)
    return call(step_kernel, out, [SMEM], VMEM)(timesteps)


def pack_kernel(cuts, *refs):
    arrays, outs, sems = refs[:3], refs[3:-1], refs[-1]
    width = arrays[0].shape[1]
    copies = []
    for index, ((cut, side, mask, _), out) in enumerate(zip(cuts, outs)):
        for which in range(out.shape[0]):
            source = arrays[which].at[:, cut(side, mask, width)]
            copies.append(pltpu.make_async_copy(source, out.at[which], sems.at[index, which]))
    for copy in copies:
        copy.start()
    for copy in copies:
        copy.wait()


def pack(cuts, arrays):
    rows, width = arrays[0].shape
    outs = tuple(
        jax.ShapeDtypeStruct(
            (count, rows, width // (4 if cut is half_columns else 8)), jnp.bfloat16
        )
        for cut, _, _, count in cuts
    )
    return call(
        functools.partial(pack_kernel, cuts),
        outs,
        [HBM] * 3,
        (VMEM,) * len(outs),
        [pltpu.SemaphoreType.DMA((len(outs), 3))],
        (0, sum(4 * out.size for out in outs), 0),
    )(*[pltpu.with_memory_space_constraint(array, pltpu.HBM) for array in arrays])


def split_kernel(got_ref, out_ref):
    out_ref[...] = got_ref[:, :, share(1, got_ref.shape[2])]


def split(got):
    count, rows, width = got.shape
    return call(
        split_kernel,
        jax.ShapeDtypeStruct((count, rows, width // 2), jnp.bfloat16),
        [VMEM],
        VMEM,
        cost=(0, 2 * got.size, 0),
    )(got)


def join_kernel(got_ref, core_ref, out_ref):
    rows = got_ref.shape[1]
    for which in range(2):
        out_ref[which, :rows] = got_ref[which, :, share(0, got_ref.shape[2])]
        out_ref[which, rows:] = core_ref[which]


def join(got, core):
    rows, size = core.shape[1:]
    return call(
        join_kernel,
        jax.ShapeDtypeStruct((2, 2 * rows, size), jnp.bfloat16),
        [VMEM] * 2,
        VMEM,
        cost=(0, 16 * rows * size, 0),
    )(got, core)


def weigh(scores, values, before=None):
    factor = LOG2E * HEAD_SIZE ** (-0.5)
    shape = (scores[0].shape[0], HEAD_SIZE)
    top = jnp.max(functools.reduce(jnp.maximum, scores), axis=-1, keepdims=True)
    top = jnp.broadcast_to(top, shape)
    if before is not None:
        top = jnp.maximum(top, before[1])
    tops = jnp.concatenate([top] * (scores[0].shape[1] // HEAD_SIZE), axis=1)
    weights = [jnp.exp2((part - tops) * factor) for part in scores]
    total = jnp.sum(functools.reduce(jnp.add, weights), axis=-1, keepdims=True)
    total = jnp.broadcast_to(total, shape)
    mixed = sum(
        jnp.dot(weight.astype(jnp.bfloat16), value, preferred_element_type=jnp.float32)
        for weight, value in zip(weights, values)
    )
    if before is not None:
        keep = jnp.exp2((before[1] - top) * factor)
        mixed = mixed + keep * before[0]
        total = total + keep * before[2]
    return mixed, top, total


def dots(query, keys):
    return [
        lax.dot_general(query, key, (((1,), (1,)), ((), ())), preferred_element_type=jnp.float32)
        for key in keys
    ]


def attend_kernel(
    side,
    keys_ref,
    values_ref,
    queries_ref,
    core_ref,
    got_ref,
    got_core_ref,
    far_ref,
    far_core_ref,
    *outs,
):
    rows, width = queries_ref.shape
    wholes = (keys_ref, values_ref, queries_ref)
    first = columns(side, 0, width).start
    tasks = [(head, pair) for head in range(core_ref.shape[2] // HEAD_SIZE) for pair in range(2)]

    def tokens(which, head):
        start = head * HEAD_SIZE
        cols = slice(start, start + HEAD_SIZE)
        mine = pl.ds(pl.multiple_of(first + start, HEAD_SIZE), HEAD_SIZE)
        ours = share(0, got_ref.shape[2], start, HEAD_SIZE)
        parts = [
            (wholes[which][:, mine], core_ref[which, :, cols]),
            (got_ref[which, :, ours], got_core_ref[which, :, cols]),
        ]
        if which < 2:
            parts.append((far_ref[which, :, ours], far_core_ref[which, :, cols]))
        return [jnp.concatenate(part) for part in parts]

    def score(head, pair):
        return dots(tokens(2, head)[pair], tokens(0, head))

    scores = score(*tasks[0])
    for index, (head, pair) in enumerate(tasks):
        following = score(*tasks[index + 1]) if index + 1 < len(tasks) else None
        cols = slice(head * HEAD_SIZE, (head + 1) * HEAD_SIZE)
        for out, value in zip(outs, weigh(scores, tokens(1, head))):
            out[2 * rows * pair : 2 * rows * (pair + 1), cols] = value
        scores = following


def attend(side, *arrays):
    rows, width = arrays[0].shape
    size = width // 8
    out = jax.ShapeDtypeStruct((4 * rows, size), jnp.float32)
    return call(
        functools.partial(attend_kernel, side),
        (out,) * 3,
        [VMEM] * 8,
        (VMEM,) * 3,
        cost=(96 * rows * rows * size, 64 * rows * size, 24 * rows * rows * size // HEAD_SIZE),
    )(*arrays)


def complete_kernel(side, queries_ref, core_ref, got_ref, got_core_ref, far_got_ref, *refs):
    old, outs = refs[:3], refs[3:]
    rows, width = queries_ref.shape
    first = columns(side, 0, width).start
    tasks = [(head, pair) for head in range(core_ref.shape[2] // HEAD_SIZE) for pair in range(2)]

    def score(head, pair):
        start = head * HEAD_SIZE
        cols = slice(start, start + HEAD_SIZE)
        if pair == 0:
            mine = pl.ds(pl.multiple_of(first + start, HEAD_SIZE), HEAD_SIZE)
            query = (queries_ref[:, mine], core_ref[2, :, cols])
        else:
            ours = share(0, got_ref.shape[2], start, HEAD_SIZE)
            query = (got_ref[2, :, ours], got_core_ref[2, :, cols])
        return dots(jnp.concatenate(query), [far_got_ref[0, :, cols]])

    scores = score(*tasks[0])
    for index, (head, pair) in enumerate(tasks):
        following = score(*tasks[index + 1]) if index + 1 < len(tasks) else None
        cols = slice(head * HEAD_SIZE, (head + 1) * HEAD_SIZE)
        before = [ref[2 * rows * pair : 2 * rows * (pair + 1), cols] for ref in old]
        mixed, _, total = weigh(scores, [far_got_ref[1, :, cols]], before)
        mixed = (mixed / total).astype(jnp.bfloat16)
        outs[2 * pair][:, cols] = mixed[:rows]
        outs[2 * pair + 1][:, cols] = mixed[rows:]
        scores = following


def complete(side, queries, core, got, far_core, far_got, old):
    rows, width = queries.shape
    size = width // 8
    out = jax.ShapeDtypeStruct((rows, size), jnp.bfloat16)
    return call(
        functools.partial(complete_kernel, side),
        (out,) * 4,
        [VMEM] * 8,
        (VMEM,) * 4,
        cost=(32 * rows * rows * size, 64 * rows * size, 8 * rows * rows * size // HEAD_SIZE),
    )(queries, core, got, far_core, far_got, *old)


def moved(latents, attended, delta):
    change = delta * attended.astype(jnp.float32)
    return (latents.astype(jnp.float32) + change).astype(jnp.bfloat16)


def lead_kernel(places, delta_ref, latents_ref, *refs):
    pieces, out_ref = refs[:-1], refs[-1]
    rows, width = latents_ref.shape
    delta = delta_ref[:, :1]
    at = 0
    for place, piece in zip(places, pieces):
        size = piece.shape[1]
        cols = columns(*place, width)
        out_ref[:, at : at + size] = moved(latents_ref[:, cols], piece[:rows], delta)
        at += size


def lead(places, delta, latents, pieces):
    rows, size = latents.shape[0], sum(piece.shape[1] for piece in pieces)
    return call(
        functools.partial(lead_kernel, places),
        jax.ShapeDtypeStruct((rows, size), jnp.bfloat16),
        [VMEM] * (2 + len(pieces)),
        VMEM,
        cost=(2 * rows * size, 6 * rows * size, 0),
    )(delta, latents, *pieces)


def finish_kernel(places, offset_ref, delta_ref, latents_ref, *refs):
    pieces = refs[: len(places)]
    attended_ref, advanced_ref, whole_ref, updated_ref, out_sem, move_sem = refs[len(places) :]
    offset, delta = offset_ref[0], delta_ref[:, :1]
    frames, rows, width = attended_ref.shape
    out_copies, move_copies = [], []
    for frame in range(frames):
        span = slice(frame * rows, (frame + 1) * rows)
        for place, piece in zip(places, pieces):
            cols = columns(*place, width)
            whole_ref[frame, :, cols] = piece[span]
        out_copies.append(
            pltpu.make_async_copy(whole_ref.at[frame], attended_ref.at[frame], out_sem.at[frame])
        )
        out_copies[-1].start()
        if frame == 0:
            continue
        updated_ref[frame] = moved(latents_ref[span], whole_ref[frame], delta)
        copy = pltpu.make_async_copy(
            updated_ref.at[frame],
            advanced_ref.at[jnp.maximum(frame - offset, 0)],
            move_sem.at[frame],
        )
        if frame < MAX_SHIFT:
            pl.when(frame >= offset)(copy.start)
        else:
            copy.start()
        move_copies.append((frame, copy))
    for copy in out_copies:
        copy.wait()
    for frame, copy in move_copies:
        if frame < MAX_SHIFT:
            pl.when(frame >= offset)(copy.wait)
        else:
            copy.wait()


def finish(shape, places, offsets, delta, latents, pieces):
    out = jax.ShapeDtypeStruct(shape, jnp.bfloat16)
    return call(
        functools.partial(finish_kernel, places),
        (out, out),
        [SMEM] + [VMEM] * (2 + len(pieces)),
        (HBM, HBM),
        [
            pltpu.VMEM(shape, jnp.bfloat16),
            pltpu.VMEM(shape, jnp.bfloat16),
            pltpu.SemaphoreType.DMA((shape[0],)),
            pltpu.SemaphoreType.DMA((shape[0],)),
        ],
        (2 * latents.size, 8 * latents.size, 0),
    )(offsets, delta, latents, *pieces)


def fill_kernel(groups, offset_ref, fresh_ref, *refs):
    leads = refs[: len(groups)]
    _, advanced_ref, coming_ref, sem = refs[len(groups) :]
    offset = offset_ref[0]
    frames, rows, width = advanced_ref.shape
    newest = lax.axis_index("queue") == lax.axis_size("queue") - 1

    @pl.when(newest)
    def _():
        coming_ref[...] = fresh_ref[...]

    @pl.when(jnp.logical_not(newest))
    def _():
        for places, part in zip(groups, leads):
            at = 0
            size = part.shape[1] // len(places)
            for place in places:
                cols = columns(*place, width)
                for frame in range(MAX_SHIFT):
                    span = slice(frame * rows, (frame + 1) * rows)
                    coming_ref[frame, :, cols] = part[span, at : at + size]
                at += size

    copies = [
        pltpu.make_async_copy(
            coming_ref.at[frame],
            advanced_ref.at[jnp.minimum(frames - offset + frame, frames - 1)],
            sem.at[frame],
        )
        for frame in range(MAX_SHIFT)
    ]
    for frame, copy in enumerate(copies):
        pl.when(frame < offset)(copy.start)
    for frame, copy in enumerate(copies):
        pl.when(frame < offset)(copy.wait)


def fill(groups, offsets, fresh, leads, advanced):
    return call(
        functools.partial(fill_kernel, groups),
        jax.ShapeDtypeStruct(advanced.shape, advanced.dtype),
        [SMEM] + [VMEM] * (1 + len(leads)) + [HBM],
        HBM,
        [pltpu.VMEM(fresh.shape, jnp.bfloat16), pltpu.SemaphoreType.DMA((MAX_SHIFT,))],
        (0, 6 * fresh.size, 0),
        input_output_aliases={2 + len(leads): 0},
    )(offsets, fresh, *leads, advanced)


def paired_shards(latents, queries, keys, values, fresh_frames, timesteps, offsets):
    shape = latents.shape[1:]
    rows = shape[0] * shape[1]
    first_rows = MAX_SHIFT * shape[1]
    width = shape[2]
    latents, queries, keys, values = (
        a.reshape(rows, width) for a in (latents, queries, keys, values)
    )
    sides = ((ACROSS, DOWN, 0), (DOWN, ACROSS, width // 2))
    arrays = (keys, values, queries)
    sends = pack([(half_columns, side, side[0], 3) for side in sides], arrays)
    owns = pack(
        [(half_columns, side, 0, 2) for side in sides]
        + [(columns, side, CORE, 3) for side in sides],
        arrays,
    )
    owns, cores = owns[: len(sides)], owns[len(sides) :]
    gots = [swapped(send, side[0]) for side, send in zip(sides, sends)]
    fars = [swapped(own, side[1]) for side, own in zip(sides, owns)]
    cores = [swapped(core, CORE) for core in cores]
    far_cores = [swapped(split(far), CORE) for far in fars]
    got_cores = [swapped(split(got), CORE) for got in gots]
    far_gots = [
        swapped(join(got, core), side[1]) for side, got, core in zip(sides, gots, got_cores)
    ]
    received = list(zip(cores, gots, got_cores, fars, far_cores))
    states = [attend(side, *arrays, *parts) for side, parts in zip(sides, received)]
    delta = step_size(timesteps)
    first_latents = latents[:first_rows]
    far_gots = [after(far, states[1 - index][0], delta) for index, far in enumerate(far_gots)]
    pieces, places, groups, leads = [], [], [], []
    for index, side in enumerate(sides):
        own, *backs = complete(
            side,
            queries,
            cores[index],
            gots[index],
            got_cores[index],
            far_gots[index],
            states[index],
        )
        groups.append([(side, mask) for mask in (0, *peers(side))])
        parts = [own] + [swapped(back, mask) for back, mask in zip(backs, peers(side))]
        head = lead(groups[-1], delta, first_latents, parts)
        leads.append(shifted(head, "queue", -1))
        pieces += parts
        places += groups[-1]
    attended, advanced = finish(shape, places, offsets, delta, latents, pieces)
    advanced = fill(groups, offsets, fresh_frames, leads, advanced)
    return (attended[None], advanced[None])


def solution(mesh):
    in_specs = (
        P("queue", None, "seq", None),
        P("queue", None, "seq", None),
        P("queue", None, "seq", None),
        P("queue", None, "seq", None),
        P(None, "seq", None),
        P(),
        P("queue"),
    )
    out_specs = (P("queue", None, "seq", None), P("queue", None, "seq", None))
    shards = paired_shards if mesh.shape["seq"] == 8 else grouped_shards
    return jax.shard_map(shards, mesh=mesh, in_specs=in_specs, out_specs=out_specs, check_vma=False)
```

```python
import functools
import jax
import jax.numpy as jnp
from jax import lax
from jax.experimental import pallas as pl
from jax.experimental.pallas import tpu as pltpu
from jax.sharding import PartitionSpec as P

HEAD_SIZE = 128
GROUPS = 8
HEAD_GRP = 3
MAX_SHIFT = 2
LOG2E = 1.4426950408889634
CORE, ACROSS, DOWN = 1, 2, 4


def shifted(block, axis, distance):
    devices = range(lax.axis_size(axis))
    route = [(i - distance, i) for i in devices if i - distance in devices]
    return lax.ppermute(block, axis, route)


def swapped(block, bit):
    return lax.ppermute(block, "seq", [(i, i ^ bit) for i in range(lax.axis_size("seq"))])


def after(block, *others):
    return lax.optimization_barrier((block, *others))[0]


def level(step, count):
    ratio = step.astype(jnp.float32) / count
    return 7.0 * ratio / (1.0 + 6.0 * ratio)


def advance(latents, attended, fresh_frames, timesteps, offsets):
    queue_count = lax.axis_size("queue")
    position = lax.axis_index("queue")
    frame_count = latents.shape[1]
    level_count = 8 * queue_count
    own_step = lax.dynamic_index_in_dim(timesteps, position, 0, keepdims=False)
    delta = 8.0 * (level(own_step - 1, level_count) - level(own_step, level_count))
    updated = (latents.astype(jnp.float32) + delta * attended.astype(jnp.float32)).astype(
        jnp.bfloat16
    )
    incoming = shifted(updated[:, :MAX_SHIFT], "queue", -1)
    incoming = jnp.where(position == queue_count - 1, fresh_frames[None], incoming)
    joined = jnp.concatenate([updated, incoming], axis=1)
    return lax.dynamic_slice_in_dim(joined, offsets[0], frame_count, 1)


def attend_items(query_part, key_part, value_part):
    length = query_part.shape[0]
    block = min(512, length)
    scale = HEAD_SIZE ** (-0.5)
    results = []
    for item in range(query_part.shape[1]):
        key_head = key_part[:, item]
        value_head = value_part[:, item]

        def one_block(query_block):
            scores = (
                jnp.einsum("qd,kd->qk", query_block, key_head, preferred_element_type=jnp.float32)
                * scale
            )
            top = jnp.max(scores, axis=-1, keepdims=True)
            weights = jnp.exp(scores - top)
            total = jnp.sum(weights, axis=-1, keepdims=True)
            mixed = (
                jnp.dot(
                    weights.astype(jnp.bfloat16), value_head, preferred_element_type=jnp.float32
                )
                / total
            )
            return mixed.astype(jnp.bfloat16)

        blocks = query_part[:, item].reshape(length // block, block, HEAD_SIZE)
        results.append(lax.map(one_block, blocks).reshape(length, HEAD_SIZE))
    return jnp.stack(results, axis=1)


def grouped_shards(latents, queries, keys, values, fresh_frames, timesteps, offsets):
    frame_count = latents.shape[1]
    frame_rows = latents.shape[2]
    seq_count = lax.axis_size("seq")
    quarters = seq_count // GROUPS
    row_count = frame_count * frame_rows
    quarter_rows = row_count // quarters
    quarter = lax.axis_index("seq") // GROUPS
    split_keys = keys.reshape(row_count, 1, GROUPS, HEAD_GRP, 1, HEAD_SIZE)
    split_values = values.reshape(row_count, 1, GROUPS, HEAD_GRP, 1, HEAD_SIZE)
    split_queries = queries.reshape(row_count, 1, GROUPS, HEAD_GRP, 1, HEAD_SIZE)
    triple = jnp.concatenate([split_queries, split_keys, split_values], axis=4)
    triple = jnp.broadcast_to(triple, (row_count, quarters, GROUPS, HEAD_GRP, 3, HEAD_SIZE))
    triple = triple.reshape(row_count, seq_count, HEAD_GRP, 3, HEAD_SIZE)
    piece = lax.all_to_all(triple, "seq", split_axis=1, concat_axis=0, tiled=True)
    items = piece.shape[2]
    query_part = piece[:, 0, :, 0].reshape(seq_count, quarter_rows, quarters, items, HEAD_SIZE)
    query_part = lax.dynamic_index_in_dim(query_part, quarter, 2, keepdims=False)
    query_part = query_part.reshape(seq_count * quarter_rows, items, HEAD_SIZE)
    outcome = attend_items(query_part, piece[:, 0, :, 1], piece[:, 0, :, 2])
    outcome = outcome.reshape(seq_count, quarter_rows, HEAD_GRP * HEAD_SIZE)
    gathered = lax.all_to_all(outcome, "seq", split_axis=0, concat_axis=2, tiled=True)
    attended = gathered.reshape(latents.shape)
    return (attended, advance(latents, attended, fresh_frames, timesteps, offsets))


VMEM_LIMIT = 16 * 1024 * 1024
VMEM = pl.BlockSpec(memory_space=pltpu.VMEM)
SMEM = pl.BlockSpec(memory_space=pltpu.SMEM)
HBM = pl.BlockSpec(memory_space=pltpu.HBM)


def call(kernel, out_shape, in_specs, out_specs, scratch_shapes=(), cost=(0, 0, 0), **options):
    return pl.pallas_call(
        kernel,
        out_shape=out_shape,
        in_specs=in_specs,
        out_specs=out_specs,
        scratch_shapes=scratch_shapes,
        cost_estimate=pl.CostEstimate(
            flops=cost[0], bytes_accessed=cost[1], transcendentals=cost[2]
        ),
        compiler_params=pltpu.CompilerParams(vmem_limit_bytes=VMEM_LIMIT),
        **options,
    )


def columns(side, mask, width):
    bit, _, base = side
    index = lax.bitwise_xor(lax.axis_index("seq"), mask)
    start = base + (index // bit) % 2 * (width // 4) + index % 2 * (width // 8)
    return pl.ds(pl.multiple_of(start, HEAD_SIZE), width // 8)


def half_columns(side, mask, width):
    bit, _, base = side
    index = lax.bitwise_xor(lax.axis_index("seq"), mask)
    start = base + (index // bit) % 2 * (width // 4)
    return pl.ds(pl.multiple_of(start, HEAD_SIZE), width // 4)


def share(other, width, skip=0, size=None):
    index = (lax.axis_index("seq") + other) % 2
    return pl.ds(pl.multiple_of(index * (width // 2) + skip, HEAD_SIZE), size or width // 2)


def peers(side):
    return (CORE, side[0], side[0] | CORE)


def step_kernel(timesteps_ref, out_ref):
    position, queue_count = lax.axis_index("queue"), lax.axis_size("queue")
    step = jnp.full(out_ref.shape, timesteps_ref[position], jnp.int32)
    out_ref[...] = 8.0 * (level(step - 1, 8 * queue_count) - level(step, 8 * queue_count))


def step_size(timesteps):
    out = jax.ShapeDtypeStruct((1, HEAD_SIZE), jnp.float32)
    return call(step_kernel, out, [SMEM], VMEM)(timesteps)


def pack_kernel(cuts, *refs):
    arrays, outs, sems = refs[:3], refs[3:-1], refs[-1]
    width = arrays[0].shape[1]
    copies = []
    for index, ((cut, side, mask, _), out) in enumerate(zip(cuts, outs)):
        for which in range(out.shape[0]):
            source = arrays[which].at[:, cut(side, mask, width)]
            copies.append(pltpu.make_async_copy(source, out.at[which], sems.at[index, which]))
    for copy in copies:
        copy.start()
    for copy in copies:
        copy.wait()


def pack(cuts, arrays):
    rows, width = arrays[0].shape
    outs = tuple(
        jax.ShapeDtypeStruct(
            (count, rows, width // (4 if cut is half_columns else 8)), jnp.bfloat16
        )
        for cut, _, _, count in cuts
    )
    return call(
        functools.partial(pack_kernel, cuts),
        outs,
        [HBM] * 3,
        (VMEM,) * len(outs),
        [pltpu.SemaphoreType.DMA((len(outs), 3))],
        (0, sum(4 * out.size for out in outs), 0),
    )(*[pltpu.with_memory_space_constraint(array, pltpu.HBM) for array in arrays])


def split_kernel(got_ref, out_ref):
    out_ref[...] = got_ref[:, :, share(1, got_ref.shape[2])]


def split(got):
    count, rows, width = got.shape
    return call(
        split_kernel,
        jax.ShapeDtypeStruct((count, rows, width // 2), jnp.bfloat16),
        [VMEM],
        VMEM,
        cost=(0, 2 * got.size, 0),
    )(got)


def join_kernel(got_ref, core_ref, out_ref):
    rows = got_ref.shape[1]
    for which in range(2):
        out_ref[which, :rows] = got_ref[which, :, share(0, got_ref.shape[2])]
        out_ref[which, rows:] = core_ref[which]


def join(got, core):
    rows, size = core.shape[1:]
    return call(
        join_kernel,
        jax.ShapeDtypeStruct((2, 2 * rows, size), jnp.bfloat16),
        [VMEM] * 2,
        VMEM,
        cost=(0, 16 * rows * size, 0),
    )(got, core)


def weigh(scores, values, before=None):
    factor = LOG2E * HEAD_SIZE ** (-0.5)
    shape = (scores[0].shape[0], HEAD_SIZE)
    top = jnp.max(functools.reduce(jnp.maximum, scores), axis=-1, keepdims=True)
    top = jnp.broadcast_to(top, shape)
    if before is not None:
        top = jnp.maximum(top, before[1])
    tops = jnp.concatenate([top] * (scores[0].shape[1] // HEAD_SIZE), axis=1)
    weights = [jnp.exp2((part - tops) * factor) for part in scores]
    total = jnp.sum(functools.reduce(jnp.add, weights), axis=-1, keepdims=True)
    total = jnp.broadcast_to(total, shape)
    mixed = sum(
        jnp.dot(weight.astype(jnp.bfloat16), value, preferred_element_type=jnp.float32)
        for weight, value in zip(weights, values)
    )
    if before is not None:
        keep = jnp.exp2((before[1] - top) * factor)
        mixed = mixed + keep * before[0]
        total = total + keep * before[2]
    return mixed, top, total


def dots(query, keys):
    return [
        lax.dot_general(query, key, (((1,), (1,)), ((), ())), preferred_element_type=jnp.float32)
        for key in keys
    ]


def attend_kernel(
    side,
    keys_ref,
    values_ref,
    queries_ref,
    core_ref,
    got_ref,
    got_core_ref,
    far_ref,
    far_core_ref,
    *outs,
):
    rows, width = queries_ref.shape
    wholes = (keys_ref, values_ref, queries_ref)
    first = columns(side, 0, width).start
    tasks = [(head, pair) for head in range(core_ref.shape[2] // HEAD_SIZE) for pair in range(2)]

    def tokens(which, head):
        start = head * HEAD_SIZE
        cols = slice(start, start + HEAD_SIZE)
        mine = pl.ds(pl.multiple_of(first + start, HEAD_SIZE), HEAD_SIZE)
        ours = share(0, got_ref.shape[2], start, HEAD_SIZE)
        parts = [
            (wholes[which][:, mine], core_ref[which, :, cols]),
            (got_ref[which, :, ours], got_core_ref[which, :, cols]),
        ]
        if which < 2:
            parts.append((far_ref[which, :, ours], far_core_ref[which, :, cols]))
        return [jnp.concatenate(part) for part in parts]

    def score(head, pair):
        return dots(tokens(2, head)[pair], tokens(0, head))

    scores = score(*tasks[0])
    for index, (head, pair) in enumerate(tasks):
        following = score(*tasks[index + 1]) if index + 1 < len(tasks) else None
        cols = slice(head * HEAD_SIZE, (head + 1) * HEAD_SIZE)
        for out, value in zip(outs, weigh(scores, tokens(1, head))):
            out[2 * rows * pair : 2 * rows * (pair + 1), cols] = value
        scores = following


def attend(side, *arrays):
    rows, width = arrays[0].shape
    size = width // 8
    out = jax.ShapeDtypeStruct((4 * rows, size), jnp.float32)
    return call(
        functools.partial(attend_kernel, side),
        (out,) * 3,
        [VMEM] * 8,
        (VMEM,) * 3,
        cost=(96 * rows * rows * size, 64 * rows * size, 24 * rows * rows * size // HEAD_SIZE),
    )(*arrays)


def complete_kernel(side, queries_ref, core_ref, got_ref, got_core_ref, far_got_ref, *refs):
    old, outs = refs[:3], refs[3:]
    rows, width = queries_ref.shape
    first = columns(side, 0, width).start
    tasks = [(head, pair) for head in range(core_ref.shape[2] // HEAD_SIZE) for pair in range(2)]

    def score(head, pair):
        start = head * HEAD_SIZE
        cols = slice(start, start + HEAD_SIZE)
        if pair == 0:
            mine = pl.ds(pl.multiple_of(first + start, HEAD_SIZE), HEAD_SIZE)
            query = (queries_ref[:, mine], core_ref[2, :, cols])
        else:
            ours = share(0, got_ref.shape[2], start, HEAD_SIZE)
            query = (got_ref[2, :, ours], got_core_ref[2, :, cols])
        return dots(jnp.concatenate(query), [far_got_ref[0, :, cols]])

    scores = score(*tasks[0])
    for index, (head, pair) in enumerate(tasks):
        following = score(*tasks[index + 1]) if index + 1 < len(tasks) else None
        cols = slice(head * HEAD_SIZE, (head + 1) * HEAD_SIZE)
        before = [ref[2 * rows * pair : 2 * rows * (pair + 1), cols] for ref in old]
        mixed, _, total = weigh(scores, [far_got_ref[1, :, cols]], before)
        mixed = (mixed / total).astype(jnp.bfloat16)
        outs[2 * pair][:, cols] = mixed[:rows]
        outs[2 * pair + 1][:, cols] = mixed[rows:]
        scores = following


def complete_both_kernel(sides, queries_ref, *refs):
    count = 7
    inputs, outs = refs[: count * len(sides)], refs[count * len(sides) :]
    core_ref, outs = outs[0], outs[1:]
    rows = queries_ref.shape[0]
    for index, side in enumerate(sides):
        own, *backs = outs[3 * index : 3 * index + 3]
        core = core_ref.at[index * rows : (index + 1) * rows]
        parts = inputs[count * index : count * (index + 1)]
        complete_kernel(side, queries_ref, *parts, own, core, *backs)


def complete(sides, queries, received):
    rows, width = queries.shape
    size = width // 8
    out = jax.ShapeDtypeStruct((rows, size), jnp.bfloat16)
    core = jax.ShapeDtypeStruct((len(sides) * rows, size), jnp.bfloat16)
    outs = call(
        functools.partial(complete_both_kernel, sides),
        (core,) + (out,) * (3 * len(sides)),
        [VMEM] * (1 + 7 * len(sides)),
        (VMEM,) * (1 + 3 * len(sides)),
        cost=(64 * rows * rows * size, 128 * rows * size, 16 * rows * rows * size // HEAD_SIZE),
    )(queries, *[part for parts in received for part in parts])
    return outs[0], [outs[3 * index + 1 : 3 * index + 4] for index in range(len(sides))]


def moved(latents, attended, delta):
    change = delta * attended.astype(jnp.float32)
    return (latents.astype(jnp.float32) + change).astype(jnp.bfloat16)


def lead_kernel(places, delta_ref, latents_ref, *refs):
    pieces, out_ref = refs[:-1], refs[-1]
    rows, width = latents_ref.shape
    delta = delta_ref[:, :1]
    at = 0
    for place, piece in zip(places, pieces):
        size = piece.shape[1]
        cols = columns(*place, width)
        out_ref[:, at : at + size] = moved(latents_ref[:, cols], piece[:rows], delta)
        at += size


def lead(places, delta, latents, pieces):
    rows, size = latents.shape[0], sum(piece.shape[1] for piece in pieces)
    return call(
        functools.partial(lead_kernel, places),
        jax.ShapeDtypeStruct((rows, size), jnp.bfloat16),
        [VMEM] * (2 + len(pieces)),
        VMEM,
        cost=(2 * rows * size, 6 * rows * size, 0),
    )(delta, latents, *pieces)


def arrive(places, offset, part_ref, advanced_ref, sems):
    frames, rows, width = advanced_ref.shape
    size = width // 8
    copies = []
    for index, place in enumerate(places):
        for frame in range(MAX_SHIFT):
            source = part_ref.at[
                frame * rows : (frame + 1) * rows, index * size : (index + 1) * size
            ]
            target = advanced_ref.at[
                jnp.minimum(frames - offset + frame, frames - 1), :, columns(*place, width)
            ]
            copy = pltpu.make_async_copy(source, target, sems.at[index, frame])
            copies.append((frame < offset, copy))
    return copies


def newest():
    return lax.axis_index("queue") == lax.axis_size("queue") - 1


def finish_kernel(places, early, offset_ref, delta_ref, latents_ref, lead_ref, *refs):
    pieces = refs[: len(places)]
    attended_ref, advanced_ref, whole_ref, updated_ref, out_sem, move_sem, lead_sem = refs[
        len(places) :
    ]
    offset, delta = offset_ref[0], delta_ref[:, :1]
    frames, rows, width = attended_ref.shape
    coming = arrive(early, offset, lead_ref, advanced_ref, lead_sem)
    for due, copy in coming:
        pl.when(jnp.logical_and(due, jnp.logical_not(newest())))(copy.start)
    out_copies, move_copies = [], []
    for frame in range(frames):
        span = slice(frame * rows, (frame + 1) * rows)
        for place, piece in zip(places, pieces):
            cols = columns(*place, width)
            whole_ref[frame, :, cols] = piece[span]
        out_copies.append(
            pltpu.make_async_copy(whole_ref.at[frame], attended_ref.at[frame], out_sem.at[frame])
        )
        out_copies[-1].start()
        if frame == 0:
            continue
        updated_ref[frame] = moved(latents_ref[span], whole_ref[frame], delta)
        copy = pltpu.make_async_copy(
            updated_ref.at[frame],
            advanced_ref.at[jnp.maximum(frame - offset, 0)],
            move_sem.at[frame],
        )
        if frame < MAX_SHIFT:
            pl.when(frame >= offset)(copy.start)
        else:
            copy.start()
        move_copies.append((frame, copy))
    for copy in out_copies:
        copy.wait()
    for frame, copy in move_copies:
        if frame < MAX_SHIFT:
            pl.when(frame >= offset)(copy.wait)
        else:
            copy.wait()
    for due, copy in coming:
        pl.when(jnp.logical_and(due, jnp.logical_not(newest())))(copy.wait)


def finish(shape, places, early, offsets, delta, latents, lead_part, pieces):
    out = jax.ShapeDtypeStruct(shape, jnp.bfloat16)
    return call(
        functools.partial(finish_kernel, places, early),
        (out, out),
        [SMEM] + [VMEM] * (3 + len(pieces)),
        (HBM, HBM),
        [
            pltpu.VMEM(shape, jnp.bfloat16),
            pltpu.VMEM(shape, jnp.bfloat16),
            pltpu.SemaphoreType.DMA((shape[0],)),
            pltpu.SemaphoreType.DMA((shape[0],)),
            pltpu.SemaphoreType.DMA((len(early), MAX_SHIFT)),
        ],
        (2 * latents.size, 8 * latents.size, 0),
    )(offsets, delta, latents, lead_part, *pieces)


def fill_kernel(groups, offset_ref, fresh_ref, *refs):
    leads, refs = refs[: len(groups)], refs[len(groups) :]
    _, advanced_ref, sems, fresh_sem = refs
    offset = offset_ref[0]
    frames = advanced_ref.shape[0]
    copies = []
    for index, (places, part) in enumerate(zip(groups, leads)):
        for due, copy in arrive(places, offset, part, advanced_ref, sems.at[index]):
            copies.append((jnp.logical_and(due, jnp.logical_not(newest())), copy))
    for frame in range(MAX_SHIFT):
        copy = pltpu.make_async_copy(
            fresh_ref.at[frame],
            advanced_ref.at[jnp.minimum(frames - offset + frame, frames - 1)],
            fresh_sem.at[frame],
        )
        copies.append((jnp.logical_and(frame < offset, newest()), copy))
    for due, copy in copies:
        pl.when(due)(copy.start)
    for due, copy in copies:
        pl.when(due)(copy.wait)


def fill(groups, offsets, fresh, leads, advanced):
    return call(
        functools.partial(fill_kernel, groups),
        jax.ShapeDtypeStruct(advanced.shape, advanced.dtype),
        [SMEM] + [VMEM] * (1 + len(leads)) + [HBM],
        HBM,
        [
            pltpu.SemaphoreType.DMA((len(groups), len(groups[0]), MAX_SHIFT)),
            pltpu.SemaphoreType.DMA((MAX_SHIFT,)),
        ],
        (0, 6 * fresh.size, 0),
        input_output_aliases={2 + len(leads): 0},
    )(offsets, fresh, *leads, advanced)


def paired_shards(latents, queries, keys, values, fresh_frames, timesteps, offsets):
    shape = latents.shape[1:]
    rows = shape[0] * shape[1]
    first_rows = MAX_SHIFT * shape[1]
    width = shape[2]
    latents, queries, keys, values = (
        a.reshape(rows, width) for a in (latents, queries, keys, values)
    )
    sides = ((ACROSS, DOWN, 0), (DOWN, ACROSS, width // 2))
    arrays = (keys, values, queries)
    sends = pack([(half_columns, side, side[0], 3) for side in sides], arrays)
    owns = pack(
        [(half_columns, side, 0, 2) for side in sides]
        + [(columns, side, CORE, 3) for side in sides],
        arrays,
    )
    owns, cores = owns[: len(sides)], owns[len(sides) :]
    gots = [swapped(send, side[0]) for send, side in zip(sends, sides)]
    cores = [swapped(core, CORE) for core in cores]
    got_cores = [swapped(split(got), CORE) for got in gots]
    fars = [swapped(own, side[1]) for side, own in zip(sides, owns)]
    far_cores = [swapped(split(far), CORE) for far in fars]
    far_gots = [
        swapped(join(got, core), side[1]) for side, got, core in zip(sides, gots, got_cores)
    ]
    received = zip(cores, gots, got_cores, fars, far_cores)
    states = [attend(side, *arrays, *parts) for side, parts in zip(sides, received)]
    delta = step_size(timesteps)
    first_latents = latents[:first_rows]
    far_gots = [after(far, states[1 - index][0], delta) for index, far in enumerate(far_gots)]
    core_out, results = complete(
        sides,
        queries,
        [
            (cores[index], gots[index], got_cores[index], far_gots[index], *states[index])
            for index in range(len(sides))
        ],
    )
    core_back = swapped(core_out, CORE)
    near_places, near_pieces, far_places, far_pieces = [], [], [], []
    for index, (side, (own, *backs)) in enumerate(zip(sides, results)):
        near_places += [(side, 0), (side, CORE)]
        near_pieces += [own, core_back[index * rows : (index + 1) * rows]]
        far_places += [(side, mask) for mask in peers(side)[1:]]
        far_pieces += [swapped(back, mask) for back, mask in zip(backs, peers(side)[1:])]
    early = shifted(lead(near_places, delta, first_latents, near_pieces), "queue", -1)
    groups = [far_places[:2], far_places[2:]]
    late = [
        shifted(lead(group, delta, first_latents, far_pieces[at : at + 2]), "queue", -1)
        for group, at in zip(groups, (0, 2))
    ]
    attended, advanced = finish(
        shape,
        near_places + far_places,
        near_places,
        offsets,
        delta,
        latents,
        early,
        near_pieces + far_pieces,
    )
    advanced = fill(groups, offsets, fresh_frames, late, advanced)
    return (attended[None], advanced[None])


def solution(mesh):
    in_specs = (
        P("queue", None, "seq", None),
        P("queue", None, "seq", None),
        P("queue", None, "seq", None),
        P("queue", None, "seq", None),
        P(None, "seq", None),
        P(),
        P("queue"),
    )
    out_specs = (P("queue", None, "seq", None), P("queue", None, "seq", None))
    shards = paired_shards if mesh.shape["seq"] == 8 else grouped_shards
    return jax.shard_map(shards, mesh=mesh, in_specs=in_specs, out_specs=out_specs, check_vma=False)
```

```python
import functools
import jax
import jax.numpy as jnp
from jax import lax
from jax.experimental import pallas as pl
from jax.experimental.pallas import tpu as pltpu
from jax.sharding import PartitionSpec as P

HEAD_SIZE = 128
GROUPS = 8
HEAD_GRP = 3
MAX_SHIFT = 2
LOG2E = 1.4426950408889634
CORE, ACROSS, DOWN = 1, 2, 4


def shifted(block, axis, distance):
    devices = range(lax.axis_size(axis))
    route = [(i - distance, i) for i in devices if i - distance in devices]
    return lax.ppermute(block, axis, route)


def swapped(block, bit):
    return lax.ppermute(block, "seq", [(i, i ^ bit) for i in range(lax.axis_size("seq"))])


def crossed(block, turn, other=0):
    bits = (ACROSS, DOWN) if turn == 0 else (DOWN, ACROSS)
    devices = range(lax.axis_size("seq"))
    return lax.ppermute(block, "seq", [(i, i ^ bits[i % 2] ^ other) for i in devices])


def after(block, *others):
    return lax.optimization_barrier((block, *others))[0]


def level(step, count):
    ratio = step.astype(jnp.float32) / count
    return 7.0 * ratio / (1.0 + 6.0 * ratio)


def advance(latents, attended, fresh_frames, timesteps, offsets):
    queue_count = lax.axis_size("queue")
    position = lax.axis_index("queue")
    frame_count = latents.shape[1]
    level_count = 8 * queue_count
    own_step = lax.dynamic_index_in_dim(timesteps, position, 0, keepdims=False)
    delta = 8.0 * (level(own_step - 1, level_count) - level(own_step, level_count))
    updated = (latents.astype(jnp.float32) + delta * attended.astype(jnp.float32)).astype(
        jnp.bfloat16
    )
    incoming = shifted(updated[:, :MAX_SHIFT], "queue", -1)
    incoming = jnp.where(position == queue_count - 1, fresh_frames[None], incoming)
    joined = jnp.concatenate([updated, incoming], axis=1)
    return lax.dynamic_slice_in_dim(joined, offsets[0], frame_count, 1)


def attend_items(query_part, key_part, value_part):
    length = query_part.shape[0]
    block = min(512, length)
    scale = HEAD_SIZE ** (-0.5)
    results = []
    for item in range(query_part.shape[1]):
        key_head = key_part[:, item]
        value_head = value_part[:, item]

        def one_block(query_block):
            scores = (
                jnp.einsum("qd,kd->qk", query_block, key_head, preferred_element_type=jnp.float32)
                * scale
            )
            top = jnp.max(scores, axis=-1, keepdims=True)
            weights = jnp.exp(scores - top)
            total = jnp.sum(weights, axis=-1, keepdims=True)
            mixed = (
                jnp.dot(
                    weights.astype(jnp.bfloat16), value_head, preferred_element_type=jnp.float32
                )
                / total
            )
            return mixed.astype(jnp.bfloat16)

        blocks = query_part[:, item].reshape(length // block, block, HEAD_SIZE)
        results.append(lax.map(one_block, blocks).reshape(length, HEAD_SIZE))
    return jnp.stack(results, axis=1)


def grouped_shards(latents, queries, keys, values, fresh_frames, timesteps, offsets):
    frame_count = latents.shape[1]
    frame_rows = latents.shape[2]
    seq_count = lax.axis_size("seq")
    quarters = seq_count // GROUPS
    row_count = frame_count * frame_rows
    quarter_rows = row_count // quarters
    quarter = lax.axis_index("seq") // GROUPS
    split_keys = keys.reshape(row_count, 1, GROUPS, HEAD_GRP, 1, HEAD_SIZE)
    split_values = values.reshape(row_count, 1, GROUPS, HEAD_GRP, 1, HEAD_SIZE)
    split_queries = queries.reshape(row_count, 1, GROUPS, HEAD_GRP, 1, HEAD_SIZE)
    triple = jnp.concatenate([split_queries, split_keys, split_values], axis=4)
    triple = jnp.broadcast_to(triple, (row_count, quarters, GROUPS, HEAD_GRP, 3, HEAD_SIZE))
    triple = triple.reshape(row_count, seq_count, HEAD_GRP, 3, HEAD_SIZE)
    piece = lax.all_to_all(triple, "seq", split_axis=1, concat_axis=0, tiled=True)
    items = piece.shape[2]
    query_part = piece[:, 0, :, 0].reshape(seq_count, quarter_rows, quarters, items, HEAD_SIZE)
    query_part = lax.dynamic_index_in_dim(query_part, quarter, 2, keepdims=False)
    query_part = query_part.reshape(seq_count * quarter_rows, items, HEAD_SIZE)
    outcome = attend_items(query_part, piece[:, 0, :, 1], piece[:, 0, :, 2])
    outcome = outcome.reshape(seq_count, quarter_rows, HEAD_GRP * HEAD_SIZE)
    gathered = lax.all_to_all(outcome, "seq", split_axis=0, concat_axis=2, tiled=True)
    attended = gathered.reshape(latents.shape)
    return (attended, advance(latents, attended, fresh_frames, timesteps, offsets))


VMEM_LIMIT = 16 * 1024 * 1024
VMEM = pl.BlockSpec(memory_space=pltpu.VMEM)
SMEM = pl.BlockSpec(memory_space=pltpu.SMEM)
HBM = pl.BlockSpec(memory_space=pltpu.HBM)


def call(kernel, out_shape, in_specs, out_specs, scratch_shapes=(), cost=(0, 0, 0), **options):
    return pl.pallas_call(
        kernel,
        out_shape=out_shape,
        in_specs=in_specs,
        out_specs=out_specs,
        scratch_shapes=scratch_shapes,
        cost_estimate=pl.CostEstimate(
            flops=cost[0], bytes_accessed=cost[1], transcendentals=cost[2]
        ),
        compiler_params=pltpu.CompilerParams(vmem_limit_bytes=VMEM_LIMIT),
        **options,
    )


def columns(side, mask, width):
    if side is None:
        return turn_columns(*mask, width)
    bit, _, base = side
    index = lax.bitwise_xor(lax.axis_index("seq"), mask)
    start = base + (index // bit) % 2 * (width // 4) + index % 2 * (width // 8)
    return pl.ds(pl.multiple_of(start, HEAD_SIZE), width // 8)


def turn_columns(turn, other, width):
    index = lax.axis_index("seq")
    first = (index + other) % 2 == turn
    index = lax.bitwise_xor(index, jnp.where(first, ACROSS, DOWN))
    index = lax.bitwise_xor(index, other)
    half = jnp.where(first, index // ACROSS % 2, 2 + index // DOWN % 2)
    start = half * (width // 4) + index % 2 * (width // 8)
    return pl.ds(pl.multiple_of(start, HEAD_SIZE), width // 8)


def half_columns(side, mask, width):
    bit, _, base = side
    index = lax.bitwise_xor(lax.axis_index("seq"), mask)
    start = base + (index // bit) % 2 * (width // 4)
    return pl.ds(pl.multiple_of(start, HEAD_SIZE), width // 4)


def send_columns(turn, mask, width):
    index = lax.axis_index("seq")
    first = 1 - (index // ACROSS) % 2
    second = 1 - (index // DOWN) % 2
    start = jnp.where(index % 2 == turn, first, 2 + second) * (width // 4)
    return pl.ds(pl.multiple_of(start, HEAD_SIZE), width // 4)


def share(other, width, skip=0, size=None):
    index = (lax.axis_index("seq") + other) % 2
    return pl.ds(pl.multiple_of(index * (width // 2) + skip, HEAD_SIZE), size or width // 2)


def peers(side):
    return (CORE, side[0], side[0] | CORE)


def step_kernel(timesteps_ref, out_ref):
    position, queue_count = lax.axis_index("queue"), lax.axis_size("queue")
    step = jnp.full(out_ref.shape, timesteps_ref[position], jnp.int32)
    out_ref[...] = 8.0 * (level(step - 1, 8 * queue_count) - level(step, 8 * queue_count))


def step_size(timesteps):
    out = jax.ShapeDtypeStruct((1, HEAD_SIZE), jnp.float32)
    return call(step_kernel, out, [SMEM], VMEM)(timesteps)


def pack_kernel(cuts, *refs):
    arrays, outs, sems = refs[:3], refs[3:-1], refs[-1]
    width = arrays[0].shape[1]
    copies = []
    for index, ((cut, side, mask, _), out) in enumerate(zip(cuts, outs)):
        for which in range(out.shape[0]):
            source = arrays[which].at[:, cut(side, mask, width)]
            copies.append(pltpu.make_async_copy(source, out.at[which], sems.at[index, which]))
    for copy in copies:
        copy.start()
    for copy in copies:
        copy.wait()


def pack(cuts, arrays):
    rows, width = arrays[0].shape
    outs = tuple(
        jax.ShapeDtypeStruct(
            (count, rows, width // (8 if cut is columns else 4)), jnp.bfloat16
        )
        for cut, _, _, count in cuts
    )
    return call(
        functools.partial(pack_kernel, cuts),
        outs,
        [HBM] * 3,
        (VMEM,) * len(outs),
        [pltpu.SemaphoreType.DMA((len(outs), 3))],
        (0, sum(4 * out.size for out in outs), 0),
    )(*[pltpu.with_memory_space_constraint(array, pltpu.HBM) for array in arrays])


def sort_kernel(*refs):
    turns, outs = refs[:2], refs[2:]
    core = lax.axis_index("seq") % 2
    for parity in range(2):

        @pl.when(core == parity)
        def _():
            for index, out in enumerate(outs):
                out[...] = turns[(index + parity) % 2][...]


def sort(*turns):
    return call(
        sort_kernel,
        tuple(jax.ShapeDtypeStruct(turn.shape, turn.dtype) for turn in turns),
        [VMEM] * 2,
        (VMEM,) * 2,
        cost=(0, 8 * turns[0].size, 0),
    )(*turns)


def split_kernel(got_ref, out_ref):
    out_ref[...] = got_ref[:, :, share(1, got_ref.shape[2])]


def split(got):
    count, rows, width = got.shape
    return call(
        split_kernel,
        jax.ShapeDtypeStruct((count, rows, width // 2), jnp.bfloat16),
        [VMEM],
        VMEM,
        cost=(0, 2 * got.size, 0),
    )(got)


def join_kernel(got_ref, core_ref, out_ref):
    rows = got_ref.shape[1]
    for which in range(2):
        out_ref[which, :rows] = got_ref[which, :, share(0, got_ref.shape[2])]
        out_ref[which, rows:] = core_ref[which]


def join(got, core):
    rows, size = core.shape[1:]
    return call(
        join_kernel,
        jax.ShapeDtypeStruct((2, 2 * rows, size), jnp.bfloat16),
        [VMEM] * 2,
        VMEM,
        cost=(0, 16 * rows * size, 0),
    )(got, core)


def weigh(scores, values, before=None):
    factor = LOG2E * HEAD_SIZE ** (-0.5)
    shape = (scores[0].shape[0], HEAD_SIZE)
    top = jnp.max(functools.reduce(jnp.maximum, scores), axis=-1, keepdims=True)
    top = jnp.broadcast_to(top, shape)
    if before is not None:
        top = jnp.maximum(top, before[1])
    tops = jnp.concatenate([top] * (scores[0].shape[1] // HEAD_SIZE), axis=1)
    weights = [jnp.exp2((part - tops) * factor) for part in scores]
    total = jnp.sum(functools.reduce(jnp.add, weights), axis=-1, keepdims=True)
    total = jnp.broadcast_to(total, shape)
    mixed = sum(
        jnp.dot(weight.astype(jnp.bfloat16), value, preferred_element_type=jnp.float32)
        for weight, value in zip(weights, values)
    )
    if before is not None:
        keep = jnp.exp2((before[1] - top) * factor)
        mixed = mixed + keep * before[0]
        total = total + keep * before[2]
    return mixed, top, total


def dots(query, keys):
    return [
        lax.dot_general(query, key, (((1,), (1,)), ((), ())), preferred_element_type=jnp.float32)
        for key in keys
    ]


def attend_kernel(
    side,
    keys_ref,
    values_ref,
    queries_ref,
    core_ref,
    got_ref,
    got_core_ref,
    far_ref,
    far_core_ref,
    *outs,
):
    rows, width = queries_ref.shape
    wholes = (keys_ref, values_ref, queries_ref)
    first = columns(side, 0, width).start
    tasks = [(head, pair) for head in range(core_ref.shape[2] // HEAD_SIZE) for pair in range(2)]

    def tokens(which, head):
        start = head * HEAD_SIZE
        cols = slice(start, start + HEAD_SIZE)
        mine = pl.ds(pl.multiple_of(first + start, HEAD_SIZE), HEAD_SIZE)
        ours = share(0, got_ref.shape[2], start, HEAD_SIZE)
        parts = [
            (wholes[which][:, mine], core_ref[which, :, cols]),
            (got_ref[which, :, ours], got_core_ref[which, :, cols]),
        ]
        if which < 2:
            parts.append((far_ref[which, :, ours], far_core_ref[which, :, cols]))
        return [jnp.concatenate(part) for part in parts]

    def score(head, pair):
        return dots(tokens(2, head)[pair], tokens(0, head))

    scores = score(*tasks[0])
    for index, (head, pair) in enumerate(tasks):
        following = score(*tasks[index + 1]) if index + 1 < len(tasks) else None
        cols = slice(head * HEAD_SIZE, (head + 1) * HEAD_SIZE)
        for out, value in zip(outs, weigh(scores, tokens(1, head))):
            out[2 * rows * pair : 2 * rows * (pair + 1), cols] = value
        scores = following


def attend(side, *arrays):
    rows, width = arrays[0].shape
    size = width // 8
    out = jax.ShapeDtypeStruct((4 * rows, size), jnp.float32)
    return call(
        functools.partial(attend_kernel, side),
        (out,) * 3,
        [VMEM] * 8,
        (VMEM,) * 3,
        cost=(96 * rows * rows * size, 64 * rows * size, 24 * rows * rows * size // HEAD_SIZE),
    )(*arrays)


def complete_kernel(side, queries_ref, core_ref, got_ref, got_core_ref, far_got_ref, *refs):
    old, outs = refs[:3], refs[3:]
    rows, width = queries_ref.shape
    first = columns(side, 0, width).start
    tasks = [(head, pair) for head in range(core_ref.shape[2] // HEAD_SIZE) for pair in range(2)]

    def score(head, pair):
        start = head * HEAD_SIZE
        cols = slice(start, start + HEAD_SIZE)
        if pair == 0:
            mine = pl.ds(pl.multiple_of(first + start, HEAD_SIZE), HEAD_SIZE)
            query = (queries_ref[:, mine], core_ref[2, :, cols])
        else:
            ours = share(0, got_ref.shape[2], start, HEAD_SIZE)
            query = (got_ref[2, :, ours], got_core_ref[2, :, cols])
        return dots(jnp.concatenate(query), [far_got_ref[0, :, cols]])

    scores = score(*tasks[0])
    for index, (head, pair) in enumerate(tasks):
        following = score(*tasks[index + 1]) if index + 1 < len(tasks) else None
        cols = slice(head * HEAD_SIZE, (head + 1) * HEAD_SIZE)
        before = [ref[2 * rows * pair : 2 * rows * (pair + 1), cols] for ref in old]
        mixed, _, total = weigh(scores, [far_got_ref[1, :, cols]], before)
        mixed = (mixed / total).astype(jnp.bfloat16)
        outs[2 * pair][:, cols] = mixed[:rows]
        outs[2 * pair + 1][:, cols] = mixed[rows:]
        scores = following


def complete_both_kernel(sides, queries_ref, *refs):
    count = 7
    inputs, outs = refs[: count * len(sides)], refs[count * len(sides) :]
    core_ref, *turn_refs = outs[:3]
    rows = queries_ref.shape[0]
    for index, side in enumerate(sides):
        turn = (lax.axis_index("seq") + index) % 2
        core = core_ref.at[index * rows : (index + 1) * rows]
        parts = inputs[count * index : count * (index + 1)]
        backs = [ref.at[turn] for ref in turn_refs]
        complete_kernel(side, queries_ref, *parts, outs[3 + index], core, *backs)


def complete(sides, queries, received):
    rows, width = queries.shape
    size = width // 8
    out = jax.ShapeDtypeStruct((rows, size), jnp.bfloat16)
    core = jax.ShapeDtypeStruct((len(sides) * rows, size), jnp.bfloat16)
    turn = jax.ShapeDtypeStruct((len(sides), rows, size), jnp.bfloat16)
    return call(
        functools.partial(complete_both_kernel, sides),
        (core, turn, turn) + (out,) * len(sides),
        [VMEM] * (1 + 7 * len(sides)),
        (VMEM,) * (3 + len(sides)),
        cost=(64 * rows * rows * size, 128 * rows * size, 16 * rows * rows * size // HEAD_SIZE),
    )(queries, *[part for parts in received for part in parts])


def moved(latents, attended, delta):
    change = delta * attended.astype(jnp.float32)
    return (latents.astype(jnp.float32) + change).astype(jnp.bfloat16)


def lead_kernel(places, delta_ref, latents_ref, *refs):
    pieces, out_ref = refs[:-1], refs[-1]
    rows, width = latents_ref.shape
    delta = delta_ref[:, :1]
    at = 0
    for place, piece in zip(places, pieces):
        size = piece.shape[1]
        cols = columns(*place, width)
        out_ref[:, at : at + size] = moved(latents_ref[:, cols], piece[:rows], delta)
        at += size


def lead(places, delta, latents, pieces):
    rows, size = latents.shape[0], sum(piece.shape[1] for piece in pieces)
    return call(
        functools.partial(lead_kernel, places),
        jax.ShapeDtypeStruct((rows, size), jnp.bfloat16),
        [VMEM] * (2 + len(pieces)),
        VMEM,
        cost=(2 * rows * size, 6 * rows * size, 0),
    )(delta, latents, *pieces)


def arrive(places, offset, part_ref, advanced_ref, sems):
    frames, rows, width = advanced_ref.shape
    size = width // 8
    copies = []
    for index, place in enumerate(places):
        for frame in range(MAX_SHIFT):
            source = part_ref.at[
                frame * rows : (frame + 1) * rows, index * size : (index + 1) * size
            ]
            target = advanced_ref.at[
                jnp.minimum(frames - offset + frame, frames - 1), :, columns(*place, width)
            ]
            copy = pltpu.make_async_copy(source, target, sems.at[index, frame])
            copies.append((frame < offset, copy))
    return copies


def newest():
    return lax.axis_index("queue") == lax.axis_size("queue") - 1


def finish_kernel(places, early, offset_ref, delta_ref, latents_ref, lead_ref, *refs):
    pieces = refs[: len(places)]
    attended_ref, advanced_ref, whole_ref, updated_ref, out_sem, move_sem, lead_sem = refs[
        len(places) :
    ]
    offset, delta = offset_ref[0], delta_ref[:, :1]
    frames, rows, width = attended_ref.shape
    coming = arrive(early, offset, lead_ref, advanced_ref, lead_sem)
    for due, copy in coming:
        pl.when(jnp.logical_and(due, jnp.logical_not(newest())))(copy.start)
    out_copies, move_copies = [], []
    for frame in range(frames):
        span = slice(frame * rows, (frame + 1) * rows)
        for place, piece in zip(places, pieces):
            cols = columns(*place, width)
            whole_ref[frame, :, cols] = piece[span]
        out_copies.append(
            pltpu.make_async_copy(whole_ref.at[frame], attended_ref.at[frame], out_sem.at[frame])
        )
        out_copies[-1].start()
        if frame == 0:
            continue
        updated_ref[frame] = moved(latents_ref[span], whole_ref[frame], delta)
        copy = pltpu.make_async_copy(
            updated_ref.at[frame],
            advanced_ref.at[jnp.maximum(frame - offset, 0)],
            move_sem.at[frame],
        )
        if frame < MAX_SHIFT:
            pl.when(frame >= offset)(copy.start)
        else:
            copy.start()
        move_copies.append((frame, copy))
    for copy in out_copies:
        copy.wait()
    for frame, copy in move_copies:
        if frame < MAX_SHIFT:
            pl.when(frame >= offset)(copy.wait)
        else:
            copy.wait()
    for due, copy in coming:
        pl.when(jnp.logical_and(due, jnp.logical_not(newest())))(copy.wait)


def finish(shape, places, early, offsets, delta, latents, lead_part, pieces):
    out = jax.ShapeDtypeStruct(shape, jnp.bfloat16)
    return call(
        functools.partial(finish_kernel, places, early),
        (out, out),
        [SMEM] + [VMEM] * (3 + len(pieces)),
        (HBM, HBM),
        [
            pltpu.VMEM(shape, jnp.bfloat16),
            pltpu.VMEM(shape, jnp.bfloat16),
            pltpu.SemaphoreType.DMA((shape[0],)),
            pltpu.SemaphoreType.DMA((shape[0],)),
            pltpu.SemaphoreType.DMA((len(early), MAX_SHIFT)),
        ],
        (2 * latents.size, 8 * latents.size, 0),
    )(offsets, delta, latents, lead_part, *pieces)


def fill_kernel(groups, offset_ref, fresh_ref, *refs):
    leads, refs = refs[: len(groups)], refs[len(groups) :]
    _, advanced_ref, sems, fresh_sem = refs
    offset = offset_ref[0]
    frames = advanced_ref.shape[0]
    copies = []
    for index, (places, part) in enumerate(zip(groups, leads)):
        for due, copy in arrive(places, offset, part, advanced_ref, sems.at[index]):
            copies.append((jnp.logical_and(due, jnp.logical_not(newest())), copy))
    for frame in range(MAX_SHIFT):
        copy = pltpu.make_async_copy(
            fresh_ref.at[frame],
            advanced_ref.at[jnp.minimum(frames - offset + frame, frames - 1)],
            fresh_sem.at[frame],
        )
        copies.append((jnp.logical_and(frame < offset, newest()), copy))
    for due, copy in copies:
        pl.when(due)(copy.start)
    for due, copy in copies:
        pl.when(due)(copy.wait)


def fill(groups, offsets, fresh, leads, advanced):
    return call(
        functools.partial(fill_kernel, groups),
        jax.ShapeDtypeStruct(advanced.shape, advanced.dtype),
        [SMEM] + [VMEM] * (1 + len(leads)) + [HBM],
        HBM,
        [
            pltpu.SemaphoreType.DMA((len(groups), len(groups[0]), MAX_SHIFT)),
            pltpu.SemaphoreType.DMA((MAX_SHIFT,)),
        ],
        (0, 6 * fresh.size, 0),
        input_output_aliases={2 + len(leads): 0},
    )(offsets, fresh, *leads, advanced)


def paired_shards(latents, queries, keys, values, fresh_frames, timesteps, offsets):
    shape = latents.shape[1:]
    rows = shape[0] * shape[1]
    first_rows = MAX_SHIFT * shape[1]
    width = shape[2]
    latents, queries, keys, values = (
        a.reshape(rows, width) for a in (latents, queries, keys, values)
    )
    sides = ((ACROSS, DOWN, 0), (DOWN, ACROSS, width // 2))
    arrays = (keys, values, queries)
    sends = pack([(send_columns, turn, 0, 3) for turn in range(len(sides))], arrays)
    owns = pack(
        [(half_columns, side, 0, 2) for side in sides]
        + [(columns, side, CORE, 3) for side in sides],
        arrays,
    )
    owns, cores = owns[: len(sides)], owns[len(sides) :]
    turns = [crossed(send, turn) for turn, send in enumerate(sends)]
    gots = sort(*turns)
    cores = [swapped(core, CORE) for core in cores]
    got_cores = [swapped(split(got), CORE) for got in gots]
    fars = [swapped(own, side[1]) for side, own in zip(sides, owns)]
    far_cores = [swapped(split(far), CORE) for far in fars]
    far_gots = [
        swapped(join(got, core), side[1]) for side, got, core in zip(sides, gots, got_cores)
    ]
    received = zip(cores, gots, got_cores, fars, far_cores)
    states = [attend(side, *arrays, *parts) for side, parts in zip(sides, received)]
    delta = step_size(timesteps)
    first_latents = latents[:first_rows]
    far_gots = [after(far, states[1 - index][0], delta) for index, far in enumerate(far_gots)]
    core_out, alike, unlike, *results = complete(
        sides,
        queries,
        [
            (cores[index], gots[index], got_cores[index], far_gots[index], *states[index])
            for index in range(len(sides))
        ],
    )
    core_back = swapped(core_out, CORE)
    near_places, near_pieces, far_places, far_pieces = [], [], [], []
    for index, (side, own) in enumerate(zip(sides, results)):
        near_places += [(side, 0), (side, CORE)]
        near_pieces += [own, core_back[index * rows : (index + 1) * rows]]
        far_places += [(None, (index, 0)), (None, (index, CORE))]
        far_pieces += [crossed(alike[index], index), crossed(unlike[index], index, CORE)]
    early = shifted(lead(near_places, delta, first_latents, near_pieces), "queue", -1)
    groups = [far_places[:2], far_places[2:]]
    late = [
        shifted(lead(group, delta, first_latents, far_pieces[at : at + 2]), "queue", -1)
        for group, at in zip(groups, (0, 2))
    ]
    attended, advanced = finish(
        shape,
        near_places + far_places,
        near_places,
        offsets,
        delta,
        latents,
        early,
        near_pieces + far_pieces,
    )
    advanced = fill(groups, offsets, fresh_frames, late, advanced)
    return (attended[None], advanced[None])


def solution(mesh):
    in_specs = (
        P("queue", None, "seq", None),
        P("queue", None, "seq", None),
        P("queue", None, "seq", None),
        P("queue", None, "seq", None),
        P(None, "seq", None),
        P(),
        P("queue"),
    )
    out_specs = (P("queue", None, "seq", None), P("queue", None, "seq", None))
    shards = paired_shards if mesh.shape["seq"] == 8 else grouped_shards
    return jax.shard_map(shards, mesh=mesh, in_specs=in_specs, out_specs=out_specs, check_vma=False)
```

```python
import functools
import jax
import jax.numpy as jnp
from jax import lax
from jax.experimental import pallas as pl
from jax.experimental.pallas import tpu as pltpu
from jax.sharding import PartitionSpec as P

HEAD_SIZE = 128
GROUPS = 8
HEAD_GRP = 3
MAX_SHIFT = 2
LOG2E = 1.4426950408889634
CORE, ACROSS, DOWN = 1, 2, 4


def shifted(block, axis, distance):
    devices = range(lax.axis_size(axis))
    route = [(i - distance, i) for i in devices if i - distance in devices]
    return lax.ppermute(block, axis, route)


def swapped(block, bit):
    return lax.ppermute(block, "seq", [(i, i ^ bit) for i in range(lax.axis_size("seq"))])


def crossed(block, turn, other=0):
    bits = (ACROSS, DOWN) if turn == 0 else (DOWN, ACROSS)
    devices = range(lax.axis_size("seq"))
    return lax.ppermute(block, "seq", [(i, i ^ bits[i % 2] ^ other) for i in devices])


def after(block, *others):
    return lax.optimization_barrier((block, *others))[0]


def level(step, count):
    ratio = step.astype(jnp.float32) / count
    return 7.0 * ratio / (1.0 + 6.0 * ratio)


def advance(latents, attended, fresh_frames, timesteps, offsets):
    queue_count = lax.axis_size("queue")
    position = lax.axis_index("queue")
    frame_count = latents.shape[1]
    level_count = 8 * queue_count
    own_step = lax.dynamic_index_in_dim(timesteps, position, 0, keepdims=False)
    delta = 8.0 * (level(own_step - 1, level_count) - level(own_step, level_count))
    updated = (latents.astype(jnp.float32) + delta * attended.astype(jnp.float32)).astype(
        jnp.bfloat16
    )
    incoming = shifted(updated[:, :MAX_SHIFT], "queue", -1)
    incoming = jnp.where(position == queue_count - 1, fresh_frames[None], incoming)
    joined = jnp.concatenate([updated, incoming], axis=1)
    return lax.dynamic_slice_in_dim(joined, offsets[0], frame_count, 1)


def attend_items(query_part, key_part, value_part):
    length = query_part.shape[0]
    block = min(512, length)
    scale = HEAD_SIZE ** (-0.5)
    results = []
    for item in range(query_part.shape[1]):
        key_head = key_part[:, item]
        value_head = value_part[:, item]

        def one_block(query_block):
            scores = (
                jnp.einsum("qd,kd->qk", query_block, key_head, preferred_element_type=jnp.float32)
                * scale
            )
            top = jnp.max(scores, axis=-1, keepdims=True)
            weights = jnp.exp(scores - top)
            total = jnp.sum(weights, axis=-1, keepdims=True)
            mixed = (
                jnp.dot(
                    weights.astype(jnp.bfloat16), value_head, preferred_element_type=jnp.float32
                )
                / total
            )
            return mixed.astype(jnp.bfloat16)

        blocks = query_part[:, item].reshape(length // block, block, HEAD_SIZE)
        results.append(lax.map(one_block, blocks).reshape(length, HEAD_SIZE))
    return jnp.stack(results, axis=1)


def grouped_shards(latents, queries, keys, values, fresh_frames, timesteps, offsets):
    frame_count = latents.shape[1]
    frame_rows = latents.shape[2]
    seq_count = lax.axis_size("seq")
    quarters = seq_count // GROUPS
    row_count = frame_count * frame_rows
    quarter_rows = row_count // quarters
    quarter = lax.axis_index("seq") // GROUPS
    split_keys = keys.reshape(row_count, 1, GROUPS, HEAD_GRP, 1, HEAD_SIZE)
    split_values = values.reshape(row_count, 1, GROUPS, HEAD_GRP, 1, HEAD_SIZE)
    split_queries = queries.reshape(row_count, 1, GROUPS, HEAD_GRP, 1, HEAD_SIZE)
    triple = jnp.concatenate([split_queries, split_keys, split_values], axis=4)
    triple = jnp.broadcast_to(triple, (row_count, quarters, GROUPS, HEAD_GRP, 3, HEAD_SIZE))
    triple = triple.reshape(row_count, seq_count, HEAD_GRP, 3, HEAD_SIZE)
    piece = lax.all_to_all(triple, "seq", split_axis=1, concat_axis=0, tiled=True)
    items = piece.shape[2]
    query_part = piece[:, 0, :, 0].reshape(seq_count, quarter_rows, quarters, items, HEAD_SIZE)
    query_part = lax.dynamic_index_in_dim(query_part, quarter, 2, keepdims=False)
    query_part = query_part.reshape(seq_count * quarter_rows, items, HEAD_SIZE)
    outcome = attend_items(query_part, piece[:, 0, :, 1], piece[:, 0, :, 2])
    outcome = outcome.reshape(seq_count, quarter_rows, HEAD_GRP * HEAD_SIZE)
    gathered = lax.all_to_all(outcome, "seq", split_axis=0, concat_axis=2, tiled=True)
    attended = gathered.reshape(latents.shape)
    return (attended, advance(latents, attended, fresh_frames, timesteps, offsets))


VMEM_LIMIT = 16 * 1024 * 1024
VMEM = pl.BlockSpec(memory_space=pltpu.VMEM)
SMEM = pl.BlockSpec(memory_space=pltpu.SMEM)
HBM = pl.BlockSpec(memory_space=pltpu.HBM)


def call(kernel, out_shape, in_specs, out_specs, scratch_shapes=(), cost=(0, 0, 0), **options):
    return pl.pallas_call(
        kernel,
        out_shape=out_shape,
        in_specs=in_specs,
        out_specs=out_specs,
        scratch_shapes=scratch_shapes,
        cost_estimate=pl.CostEstimate(
            flops=cost[0], bytes_accessed=cost[1], transcendentals=cost[2]
        ),
        compiler_params=pltpu.CompilerParams(vmem_limit_bytes=VMEM_LIMIT),
        **options,
    )


def columns(side, mask, width):
    if side is None:
        return turn_columns(*mask, width)
    bit, _, base = side
    index = lax.bitwise_xor(lax.axis_index("seq"), mask)
    start = base + (index // bit) % 2 * (width // 4) + index % 2 * (width // 8)
    return pl.ds(pl.multiple_of(start, HEAD_SIZE), width // 8)


def turn_columns(turn, other, width):
    index = lax.axis_index("seq")
    first = (index + other) % 2 == turn
    index = lax.bitwise_xor(index, jnp.where(first, ACROSS, DOWN))
    index = lax.bitwise_xor(index, other)
    half = jnp.where(first, index // ACROSS % 2, 2 + index // DOWN % 2)
    start = half * (width // 4) + index % 2 * (width // 8)
    return pl.ds(pl.multiple_of(start, HEAD_SIZE), width // 8)


def half_columns(side, mask, width):
    bit, _, base = side
    index = lax.bitwise_xor(lax.axis_index("seq"), mask)
    start = base + (index // bit) % 2 * (width // 4)
    return pl.ds(pl.multiple_of(start, HEAD_SIZE), width // 4)


def send_columns(turn, mask, width):
    index = lax.axis_index("seq")
    first = 1 - (index // ACROSS) % 2
    second = 1 - (index // DOWN) % 2
    start = jnp.where(index % 2 == turn, first, 2 + second) * (width // 4)
    return pl.ds(pl.multiple_of(start, HEAD_SIZE), width // 4)


def share(other, width, skip=0, size=None):
    index = (lax.axis_index("seq") + other) % 2
    return pl.ds(pl.multiple_of(index * (width // 2) + skip, HEAD_SIZE), size or width // 2)


def peers(side):
    return (CORE, side[0], side[0] | CORE)


def step_kernel(timesteps_ref, out_ref):
    position, queue_count = lax.axis_index("queue"), lax.axis_size("queue")
    step = jnp.full(out_ref.shape, timesteps_ref[position], jnp.int32)
    out_ref[...] = 8.0 * (level(step - 1, 8 * queue_count) - level(step, 8 * queue_count))


def step_size(timesteps):
    out = jax.ShapeDtypeStruct((1, HEAD_SIZE), jnp.float32)
    return call(step_kernel, out, [SMEM], VMEM)(timesteps)


def pack_kernel(cuts, *refs):
    arrays, outs, sems = refs[:3], refs[3:-1], refs[-1]
    width = arrays[0].shape[1]
    copies = []
    for index, ((cut, side, mask, _), out) in enumerate(zip(cuts, outs)):
        for which in range(out.shape[0]):
            source = arrays[which].at[:, cut(side, mask, width)]
            copies.append(pltpu.make_async_copy(source, out.at[which], sems.at[index, which]))
    for copy in copies:
        copy.start()
    for copy in copies:
        copy.wait()


def pack(cuts, arrays):
    rows, width = arrays[0].shape
    outs = tuple(
        jax.ShapeDtypeStruct(
            (count, rows, width // (8 if cut is columns else 4)), jnp.bfloat16
        )
        for cut, _, _, count in cuts
    )
    return call(
        functools.partial(pack_kernel, cuts),
        outs,
        [HBM] * 3,
        (VMEM,) * len(outs),
        [pltpu.SemaphoreType.DMA((len(outs), 3))],
        (0, sum(4 * out.size for out in outs), 0),
    )(*[pltpu.with_memory_space_constraint(array, pltpu.HBM) for array in arrays])


def sort_kernel(*refs):
    turns, outs = refs[:2], refs[2:]
    core = lax.axis_index("seq") % 2
    for parity in range(2):

        @pl.when(core == parity)
        def _():
            for index, out in enumerate(outs):
                out[...] = turns[(index + parity) % 2][...]


def sort(*turns):
    return call(
        sort_kernel,
        tuple(jax.ShapeDtypeStruct(turn.shape, turn.dtype) for turn in turns),
        [VMEM] * 2,
        (VMEM,) * 2,
        cost=(0, 8 * turns[0].size, 0),
    )(*turns)


def split_kernel(got_ref, out_ref):
    out_ref[...] = got_ref[:, :, share(1, got_ref.shape[2])]


def split(got):
    count, rows, width = got.shape
    return call(
        split_kernel,
        jax.ShapeDtypeStruct((count, rows, width // 2), jnp.bfloat16),
        [VMEM],
        VMEM,
        cost=(0, 2 * got.size, 0),
    )(got)


def join_kernel(got_ref, core_ref, out_ref):
    rows = got_ref.shape[1]
    for which in range(2):
        out_ref[which, :rows] = got_ref[which, :, share(0, got_ref.shape[2])]
        out_ref[which, rows:] = core_ref[which]


def join(got, core):
    rows, size = core.shape[1:]
    return call(
        join_kernel,
        jax.ShapeDtypeStruct((2, 2 * rows, size), jnp.bfloat16),
        [VMEM] * 2,
        VMEM,
        cost=(0, 16 * rows * size, 0),
    )(got, core)


def weigh(scores, values, before=None):
    factor = LOG2E * HEAD_SIZE ** (-0.5)
    shape = (scores[0].shape[0], HEAD_SIZE)
    top = jnp.max(functools.reduce(jnp.maximum, scores), axis=-1, keepdims=True)
    top = jnp.broadcast_to(top, shape)
    if before is not None:
        top = jnp.maximum(top, before[1])
    tops = jnp.concatenate([top] * (scores[0].shape[1] // HEAD_SIZE), axis=1)
    weights = [jnp.exp2((part - tops) * factor) for part in scores]
    ones = jnp.ones(values[0].shape, jnp.bfloat16)
    mixed = sum(
        jnp.dot(
            weight.astype(jnp.bfloat16),
            jnp.concatenate([value, ones], axis=1),
            preferred_element_type=jnp.float32,
        )
        for weight, value in zip(weights, values)
    )
    mixed, total = mixed[:, :HEAD_SIZE], mixed[:, HEAD_SIZE:]
    if before is not None:
        keep = jnp.exp2((before[1] - top) * factor)
        mixed = mixed + keep * before[0]
        total = total + keep * before[2]
    return mixed, top, total


def dots(query, keys):
    return [
        lax.dot_general(query, key, (((1,), (1,)), ((), ())), preferred_element_type=jnp.float32)
        for key in keys
    ]


def attend_kernel(
    side,
    keys_ref,
    values_ref,
    queries_ref,
    core_ref,
    got_ref,
    got_core_ref,
    far_ref,
    far_core_ref,
    *outs,
):
    rows, width = queries_ref.shape
    wholes = (keys_ref, values_ref, queries_ref)
    first = columns(side, 0, width).start
    tasks = [(head, pair) for head in range(core_ref.shape[2] // HEAD_SIZE) for pair in range(2)]

    def tokens(which, head):
        start = head * HEAD_SIZE
        cols = slice(start, start + HEAD_SIZE)
        mine = pl.ds(pl.multiple_of(first + start, HEAD_SIZE), HEAD_SIZE)
        ours = share(0, got_ref.shape[2], start, HEAD_SIZE)
        parts = [
            (wholes[which][:, mine], core_ref[which, :, cols]),
            (got_ref[which, :, ours], got_core_ref[which, :, cols]),
        ]
        if which < 2:
            parts.append((far_ref[which, :, ours], far_core_ref[which, :, cols]))
        return [jnp.concatenate(part) for part in parts]

    def score(head, pair):
        return dots(tokens(2, head)[pair], tokens(0, head))

    scores = score(*tasks[0])
    for index, (head, pair) in enumerate(tasks):
        following = score(*tasks[index + 1]) if index + 1 < len(tasks) else None
        cols = slice(head * HEAD_SIZE, (head + 1) * HEAD_SIZE)
        for out, value in zip(outs, weigh(scores, tokens(1, head))):
            out[2 * rows * pair : 2 * rows * (pair + 1), cols] = value
        scores = following


def attend(side, *arrays):
    rows, width = arrays[0].shape
    size = width // 8
    out = jax.ShapeDtypeStruct((4 * rows, size), jnp.float32)
    return call(
        functools.partial(attend_kernel, side),
        (out,) * 3,
        [VMEM] * 8,
        (VMEM,) * 3,
        cost=(96 * rows * rows * size, 64 * rows * size, 24 * rows * rows * size // HEAD_SIZE),
    )(*arrays)


def complete_kernel(side, queries_ref, core_ref, got_ref, got_core_ref, far_got_ref, *refs):
    old, outs = refs[:3], refs[3:]
    rows, width = queries_ref.shape
    first = columns(side, 0, width).start
    tasks = [(head, pair) for head in range(core_ref.shape[2] // HEAD_SIZE) for pair in range(2)]

    def score(head, pair):
        start = head * HEAD_SIZE
        cols = slice(start, start + HEAD_SIZE)
        if pair == 0:
            mine = pl.ds(pl.multiple_of(first + start, HEAD_SIZE), HEAD_SIZE)
            query = (queries_ref[:, mine], core_ref[2, :, cols])
        else:
            ours = share(0, got_ref.shape[2], start, HEAD_SIZE)
            query = (got_ref[2, :, ours], got_core_ref[2, :, cols])
        return dots(jnp.concatenate(query), [far_got_ref[0, :, cols]])

    scores = score(*tasks[0])
    for index, (head, pair) in enumerate(tasks):
        following = score(*tasks[index + 1]) if index + 1 < len(tasks) else None
        cols = slice(head * HEAD_SIZE, (head + 1) * HEAD_SIZE)
        before = [ref[2 * rows * pair : 2 * rows * (pair + 1), cols] for ref in old]
        mixed, _, total = weigh(scores, [far_got_ref[1, :, cols]], before)
        mixed = (mixed / total).astype(jnp.bfloat16)
        outs[2 * pair][:, cols] = mixed[:rows]
        outs[2 * pair + 1][:, cols] = mixed[rows:]
        scores = following


def complete_both_kernel(sides, queries_ref, *refs):
    count = 7
    inputs, outs = refs[: count * len(sides)], refs[count * len(sides) :]
    core_ref, *turn_refs = outs[:3]
    rows = queries_ref.shape[0]
    for index, side in enumerate(sides):
        turn = (lax.axis_index("seq") + index) % 2
        core = core_ref.at[index * rows : (index + 1) * rows]
        parts = inputs[count * index : count * (index + 1)]
        backs = [ref.at[turn] for ref in turn_refs]
        complete_kernel(side, queries_ref, *parts, outs[3 + index], core, *backs)


def complete(sides, queries, received):
    rows, width = queries.shape
    size = width // 8
    out = jax.ShapeDtypeStruct((rows, size), jnp.bfloat16)
    core = jax.ShapeDtypeStruct((len(sides) * rows, size), jnp.bfloat16)
    turn = jax.ShapeDtypeStruct((len(sides), rows, size), jnp.bfloat16)
    return call(
        functools.partial(complete_both_kernel, sides),
        (core, turn, turn) + (out,) * len(sides),
        [VMEM] * (1 + 7 * len(sides)),
        (VMEM,) * (3 + len(sides)),
        cost=(64 * rows * rows * size, 128 * rows * size, 16 * rows * rows * size // HEAD_SIZE),
    )(queries, *[part for parts in received for part in parts])


def moved(latents, attended, delta):
    change = delta * attended.astype(jnp.float32)
    return (latents.astype(jnp.float32) + change).astype(jnp.bfloat16)


def lead_kernel(places, delta_ref, latents_ref, *refs):
    pieces, out_ref = refs[:-1], refs[-1]
    rows, width = latents_ref.shape
    delta = delta_ref[:, :1]
    at = 0
    for place, piece in zip(places, pieces):
        size = piece.shape[1]
        cols = columns(*place, width)
        out_ref[:, at : at + size] = moved(latents_ref[:, cols], piece[:rows], delta)
        at += size


def lead(places, delta, latents, pieces):
    rows, size = latents.shape[0], sum(piece.shape[1] for piece in pieces)
    return call(
        functools.partial(lead_kernel, places),
        jax.ShapeDtypeStruct((rows, size), jnp.bfloat16),
        [VMEM] * (2 + len(pieces)),
        VMEM,
        cost=(2 * rows * size, 6 * rows * size, 0),
    )(delta, latents, *pieces)


def arrive(places, offset, part_ref, advanced_ref, sems):
    frames, rows, width = advanced_ref.shape
    size = width // 8
    copies = []
    for index, place in enumerate(places):
        for frame in range(MAX_SHIFT):
            source = part_ref.at[
                frame * rows : (frame + 1) * rows, index * size : (index + 1) * size
            ]
            target = advanced_ref.at[
                jnp.minimum(frames - offset + frame, frames - 1), :, columns(*place, width)
            ]
            copy = pltpu.make_async_copy(source, target, sems.at[index, frame])
            copies.append((frame < offset, copy))
    return copies


def newest():
    return lax.axis_index("queue") == lax.axis_size("queue") - 1


def finish_kernel(places, early, offset_ref, delta_ref, latents_ref, lead_ref, *refs):
    pieces = refs[: len(places)]
    attended_ref, advanced_ref, whole_ref, updated_ref, out_sem, move_sem, lead_sem = refs[
        len(places) :
    ]
    offset, delta = offset_ref[0], delta_ref[:, :1]
    frames, rows, width = attended_ref.shape
    coming = arrive(early, offset, lead_ref, advanced_ref, lead_sem)
    for due, copy in coming:
        pl.when(jnp.logical_and(due, jnp.logical_not(newest())))(copy.start)
    out_copies, move_copies = [], []
    for frame in range(frames):
        span = slice(frame * rows, (frame + 1) * rows)
        for place, piece in zip(places, pieces):
            cols = columns(*place, width)
            whole_ref[frame, :, cols] = piece[span]
        out_copies.append(
            pltpu.make_async_copy(whole_ref.at[frame], attended_ref.at[frame], out_sem.at[frame])
        )
        out_copies[-1].start()
        if frame == 0:
            continue
        updated_ref[frame] = moved(latents_ref[span], whole_ref[frame], delta)
        copy = pltpu.make_async_copy(
            updated_ref.at[frame],
            advanced_ref.at[jnp.maximum(frame - offset, 0)],
            move_sem.at[frame],
        )
        if frame < MAX_SHIFT:
            pl.when(frame >= offset)(copy.start)
        else:
            copy.start()
        move_copies.append((frame, copy))
    for copy in out_copies:
        copy.wait()
    for frame, copy in move_copies:
        if frame < MAX_SHIFT:
            pl.when(frame >= offset)(copy.wait)
        else:
            copy.wait()
    for due, copy in coming:
        pl.when(jnp.logical_and(due, jnp.logical_not(newest())))(copy.wait)


def finish(shape, places, early, offsets, delta, latents, lead_part, pieces):
    out = jax.ShapeDtypeStruct(shape, jnp.bfloat16)
    return call(
        functools.partial(finish_kernel, places, early),
        (out, out),
        [SMEM] + [VMEM] * (3 + len(pieces)),
        (HBM, HBM),
        [
            pltpu.VMEM(shape, jnp.bfloat16),
            pltpu.VMEM(shape, jnp.bfloat16),
            pltpu.SemaphoreType.DMA((shape[0],)),
            pltpu.SemaphoreType.DMA((shape[0],)),
            pltpu.SemaphoreType.DMA((len(early), MAX_SHIFT)),
        ],
        (2 * latents.size, 8 * latents.size, 0),
    )(offsets, delta, latents, lead_part, *pieces)


def fill_kernel(groups, offset_ref, fresh_ref, *refs):
    leads, refs = refs[: len(groups)], refs[len(groups) :]
    _, advanced_ref, sems, fresh_sem = refs
    offset = offset_ref[0]
    frames = advanced_ref.shape[0]
    copies = []
    for index, (places, part) in enumerate(zip(groups, leads)):
        for due, copy in arrive(places, offset, part, advanced_ref, sems.at[index]):
            copies.append((jnp.logical_and(due, jnp.logical_not(newest())), copy))
    for frame in range(MAX_SHIFT):
        copy = pltpu.make_async_copy(
            fresh_ref.at[frame],
            advanced_ref.at[jnp.minimum(frames - offset + frame, frames - 1)],
            fresh_sem.at[frame],
        )
        copies.append((jnp.logical_and(frame < offset, newest()), copy))
    for due, copy in copies:
        pl.when(due)(copy.start)
    for due, copy in copies:
        pl.when(due)(copy.wait)


def fill(groups, offsets, fresh, leads, advanced):
    return call(
        functools.partial(fill_kernel, groups),
        jax.ShapeDtypeStruct(advanced.shape, advanced.dtype),
        [SMEM] + [VMEM] * (1 + len(leads)) + [HBM],
        HBM,
        [
            pltpu.SemaphoreType.DMA((len(groups), len(groups[0]), MAX_SHIFT)),
            pltpu.SemaphoreType.DMA((MAX_SHIFT,)),
        ],
        (0, 6 * fresh.size, 0),
        input_output_aliases={2 + len(leads): 0},
    )(offsets, fresh, *leads, advanced)


def paired_shards(latents, queries, keys, values, fresh_frames, timesteps, offsets):
    shape = latents.shape[1:]
    rows = shape[0] * shape[1]
    first_rows = MAX_SHIFT * shape[1]
    width = shape[2]
    latents, queries, keys, values = (
        a.reshape(rows, width) for a in (latents, queries, keys, values)
    )
    sides = ((ACROSS, DOWN, 0), (DOWN, ACROSS, width // 2))
    arrays = (keys, values, queries)
    sends = pack([(send_columns, turn, 0, 3) for turn in range(len(sides))], arrays)
    owns = pack(
        [(half_columns, side, 0, 2) for side in sides]
        + [(columns, side, CORE, 3) for side in sides],
        arrays,
    )
    owns, cores = owns[: len(sides)], owns[len(sides) :]
    turns = [crossed(send, turn) for turn, send in enumerate(sends)]
    gots = sort(*turns)
    cores = [swapped(core, CORE) for core in cores]
    got_cores = [swapped(split(got), CORE) for got in gots]
    fars = [swapped(own, side[1]) for side, own in zip(sides, owns)]
    far_cores = [swapped(split(far), CORE) for far in fars]
    far_gots = [
        swapped(join(got, core), side[1]) for side, got, core in zip(sides, gots, got_cores)
    ]
    received = zip(cores, gots, got_cores, fars, far_cores)
    states = [attend(side, *arrays, *parts) for side, parts in zip(sides, received)]
    delta = step_size(timesteps)
    first_latents = latents[:first_rows]
    far_gots = [after(far, states[1 - index][0], delta) for index, far in enumerate(far_gots)]
    core_out, alike, unlike, *results = complete(
        sides,
        queries,
        [
            (cores[index], gots[index], got_cores[index], far_gots[index], *states[index])
            for index in range(len(sides))
        ],
    )
    core_back = swapped(core_out, CORE)
    near_places, near_pieces, far_places, far_pieces = [], [], [], []
    for index, (side, own) in enumerate(zip(sides, results)):
        near_places += [(side, 0), (side, CORE)]
        near_pieces += [own, core_back[index * rows : (index + 1) * rows]]
        far_places += [(None, (index, 0)), (None, (index, CORE))]
        far_pieces += [crossed(alike[index], index), crossed(unlike[index], index, CORE)]
    early = shifted(lead(near_places, delta, first_latents, near_pieces), "queue", -1)
    groups = [far_places[:2], far_places[2:]]
    late = [
        shifted(lead(group, delta, first_latents, far_pieces[at : at + 2]), "queue", -1)
        for group, at in zip(groups, (0, 2))
    ]
    attended, advanced = finish(
        shape,
        near_places + far_places,
        near_places,
        offsets,
        delta,
        latents,
        early,
        near_pieces + far_pieces,
    )
    advanced = fill(groups, offsets, fresh_frames, late, advanced)
    return (attended[None], advanced[None])


def solution(mesh):
    in_specs = (
        P("queue", None, "seq", None),
        P("queue", None, "seq", None),
        P("queue", None, "seq", None),
        P("queue", None, "seq", None),
        P(None, "seq", None),
        P(),
        P("queue"),
    )
    out_specs = (P("queue", None, "seq", None), P("queue", None, "seq", None))
    shards = paired_shards if mesh.shape["seq"] == 8 else grouped_shards
    return jax.shard_map(shards, mesh=mesh, in_specs=in_specs, out_specs=out_specs, check_vma=False)
```
